256 devices in a mesh: head: 4 (over x_hi, core), inner: 16 (over x_lo, z), outer: 4 (over y).
Axes of the slice: x: 4 (x_hi: 2, x_lo: 2; x = x_hi * 2 + x_lo), y: 4, z: 8, core: 2. Of those that a mesh axis runs over, the one named last changes fastest.
Arguments:
- queries: bfloat16 [14336, 4096], P(('head', 'inner', 'outer')), may hold values from -400 to 400
- keys: bfloat16 [14336, 1024], P(('head', 'inner', 'outer')), may hold values from -14 to 14
- values: bfloat16 [14336, 1024], P(('head', 'inner', 'outer')), may hold values from -6 to 6
- span_order: int32 [256], replicated, may hold values from 0 to 255, each once
- block_pattern: int32 [256, 256], replicated, may hold values 0 or 1
- summary_flag: int32 [256], replicated, may hold values 0 or 1
Outputs:
- attended: bfloat16 [14336, 4096], P(('head', 'inner', 'outer'))
The draws below stay inside these ranges and needn't reach their ends.
All inputs are finite; a program needn't handle non-finite values.
Results may differ from the reference program's by a relative error of at most 0.0064.
Values may be sent and summed in bfloat16 or wider, within the bound.
No kernel may reach another device: no remote copies, remote signals or barrier semaphores. Data moves between devices by JAX's collectives and lax.ppermute only.
A program may use at most 64 MiB of HBM per device.

```python
import math
import jax
import jax.numpy as jnp
from jax import lax

QUERY_HEAD_COUNT = 32
KEY_VALUE_HEADS = 8
HEAD_SIZE = 128
SPAN_TOKENS = 56
SPAN_COUNT = 256
TOKEN_COUNT = 14336


def paired_fields(key, boost):
    base_random_key = jax.random.fold_in(key, 0)
    k_pick = jax.random.fold_in(key, 2)
    k_level = jax.random.fold_in(key, 3)
    noise_random_key = jax.random.fold_in(key, 4)
    k_query = jax.random.fold_in(key, 5)
    base_tensor = jax.random.truncated_normal(base_random_key, -6.0, 6.0, (TOKEN_COUNT, KEY_VALUE_HEADS * HEAD_SIZE), jnp.float32)
    row_index = jnp.arange(TOKEN_COUNT)
    chosen = (jax.random.randint(k_pick, (TOKEN_COUNT,), 0, 16) == 0) & (row_index % 2 == 1) & (boost > 0.0)
    follow = jnp.roll(chosen, -1)
    random_jitter = jax.random.truncated_normal(noise_random_key, -6.0, 6.0, (TOKEN_COUNT, KEY_VALUE_HEADS * HEAD_SIZE), jnp.float32)
    output_keys = jnp.where(follow[:, None], 0.99 * jnp.roll(base_tensor, -1, axis=0) + 0.01 * random_jitter, base_tensor)
    level = 10.0 * (1 + jax.random.randint(k_level, (TOKEN_COUNT,), 0, 3)).astype(jnp.float32)
    group_ratio = QUERY_HEAD_COUNT // KEY_VALUE_HEADS
    widened_keys = jnp.broadcast_to(output_keys.reshape(TOKEN_COUNT, KEY_VALUE_HEADS, 1, HEAD_SIZE), (TOKEN_COUNT, KEY_VALUE_HEADS, group_ratio, HEAD_SIZE)).reshape(TOKEN_COUNT, QUERY_HEAD_COUNT * HEAD_SIZE)
    drawn = 2.0 * jax.random.truncated_normal(k_query, -6.0, 6.0, (TOKEN_COUNT, QUERY_HEAD_COUNT * HEAD_SIZE), jnp.float32)
    queries_out = jnp.where(chosen[:, None], boost * level[:, None] * widened_keys, drawn)
    return (output_keys, queries_out)


def draw_keys(key, part):
    boost = 0.0
    shared = paired_fields(key, boost)[0]
    return shared.astype(jnp.bfloat16)


def draw_queries(key, part):
    boost = 0.0
    shared = paired_fields(key, boost)[1]
    return shared.astype(jnp.bfloat16)


def touch_ends(entries, stream_key, low, top_value):
    place = [jax.random.randint(jax.random.fold_in(stream_key, axis), (), 0, length) for axis, length in enumerate(entries.shape)]
    widest = entries.shape.index(max(entries.shape))
    neighbour = place[:widest] + [(place[widest] + 1) % entries.shape[widest]] + place[widest + 1:]
    return entries.at[tuple(place)].set(low).at[tuple(neighbour)].set(top_value)


def steps_of(own_key, dims, cuts, low, largest):
    gain, own = 1.0, jax.random.fold_in(own_key, 6)
    for dim, parts in cuts:
        heights = jnp.exp(jax.random.uniform(jax.random.fold_in(own, dim), (parts,), jnp.float32, low / len(cuts), largest / len(cuts)))
        gain = gain * jnp.repeat(heights, dims[dim] // parts).reshape([-1 if axis == dim else 1 for axis in range(len(dims))])
    return gain


def centred(stream_key, shape, scale, reach, cuts=(), kind=jnp.bfloat16):
    gain = steps_of(stream_key, shape, cuts, -0.22, 0.18) if cuts else 1.0
    drawn = jax.random.normal(stream_key, shape, jnp.float32) * scale * gain
    return jnp.minimum(jnp.maximum(drawn, -reach), reach).astype(kind)


def setup_inputs(seed: int = 0) -> dict:
    key_of = jax.random.split(jax.random.key(seed), 7)
    return {
        "queries": draw_queries(jax.random.fold_in(key_of[6], 71), 0),
        "keys": draw_keys(jax.random.fold_in(key_of[6], 71), 0),
        "values": centred(key_of[2], (TOKEN_COUNT, KEY_VALUE_HEADS * HEAD_SIZE), 1.0, 6.0, ((0, 256),)),
        "span_order": jax.random.permutation(key_of[3], SPAN_COUNT).astype(jnp.int32),
        "block_pattern": touch_ends((jax.random.randint(key_of[4], (SPAN_COUNT, SPAN_COUNT), 0, 8) < 1).astype(jnp.int32), jax.random.fold_in(key_of[4], 1), 0, 1),
        "summary_flag": touch_ends((jax.random.randint(key_of[5], (SPAN_COUNT,), 0, 2) < 1).astype(jnp.int32), jax.random.fold_in(key_of[5], 1), 0, 1),
    }


NEG = -1e+30
BLOCK_LIMIT = 128

def reference(queries, keys, values, span_order, block_pattern, summary_flag):
    group_ratio = QUERY_HEAD_COUNT // KEY_VALUE_HEADS
    score_scale = 1.0 / math.sqrt(HEAD_SIZE)
    summary_bias = math.log(SPAN_TOKENS)
    row_index = jnp.arange(TOKEN_COUNT, dtype=jnp.int32)
    true_span = jnp.take(span_order, row_index // SPAN_TOKENS).astype(jnp.int32)
    position = true_span * SPAN_TOKENS + row_index % SPAN_TOKENS
    key_summary_sum = (lax.optimization_barrier(jnp.sum(keys.reshape(SPAN_COUNT, SPAN_TOKENS, KEY_VALUE_HEADS * HEAD_SIZE).astype(jnp.float32), axis=1)) / math.sqrt(SPAN_TOKENS)).astype(jnp.bfloat16)
    value_summary_sum = (lax.optimization_barrier(jnp.sum(values.reshape(SPAN_COUNT, SPAN_TOKENS, KEY_VALUE_HEADS * HEAD_SIZE).astype(jnp.float32), axis=1)) / math.sqrt(SPAN_TOKENS)).astype(jnp.bfloat16)
    dense_key = keys.astype(jnp.float32).reshape(TOKEN_COUNT, KEY_VALUE_HEADS, HEAD_SIZE)
    dense_value = values.astype(jnp.float32).reshape(TOKEN_COUNT, KEY_VALUE_HEADS, HEAD_SIZE)
    compact_key = key_summary_sum.astype(jnp.float32).reshape(SPAN_COUNT, KEY_VALUE_HEADS, HEAD_SIZE)
    compact_value = value_summary_sum.astype(jnp.float32).reshape(SPAN_COUNT, KEY_VALUE_HEADS, HEAD_SIZE)
    flag_stored = jnp.take(summary_flag, span_order)
    rows_per_block = min(BLOCK_LIMIT, TOKEN_COUNT)

    def attend_rows(leading_row):
        block_of_queries = lax.dynamic_slice_in_dim(queries, leading_row, rows_per_block, 0).astype(jnp.float32).reshape(rows_per_block, KEY_VALUE_HEADS, group_ratio, HEAD_SIZE)
        query_span = lax.dynamic_slice_in_dim(true_span, leading_row, rows_per_block, 0)
        query_pos = lax.dynamic_slice_in_dim(position, leading_row, rows_per_block, 0)
        pattern_rows = jnp.take(block_pattern, query_span, axis=0)
        full_pattern = jnp.take(pattern_rows, true_span, axis=1)
        same_span = (query_span[:, None] == true_span[None, :]) & (position[None, :] <= query_pos[:, None])
        earlier = true_span[None, :] < query_span[:, None]
        allowed = same_span | earlier & (full_pattern == 1)
        short_pattern = jnp.take(pattern_rows, span_order, axis=1)
        short_allowed = (span_order[None, :] < query_span[:, None]) & (short_pattern == 0) & (flag_stored[None, :] == 1)
        scores = jnp.einsum('qhgd,khd->qhgk', block_of_queries, dense_key) * score_scale
        short_scores = jnp.einsum('qhgd,khd->qhgk', block_of_queries, compact_key) * score_scale + summary_bias
        scores = jnp.where(allowed[:, None, None, :], scores, NEG)
        short_scores = jnp.where(short_allowed[:, None, None, :], short_scores, NEG)
        row_peak = jnp.maximum(scores.max(-1), short_scores.max(-1))
        weights = jnp.where(allowed[:, None, None, :], jnp.exp(scores - row_peak[..., None]), 0.0)
        short_weights = jnp.where(short_allowed[:, None, None, :], jnp.exp(short_scores - row_peak[..., None]), 0.0)
        row_total = weights.sum(-1) + short_weights.sum(-1)
        rounded = lax.optimization_barrier(weights.astype(jnp.bfloat16)).astype(jnp.float32)
        short_rounded = lax.optimization_barrier(short_weights.astype(jnp.bfloat16)).astype(jnp.float32)
        mixed = jnp.einsum('qhgk,khd->qhgd', rounded, dense_value) + jnp.einsum('qhgk,khd->qhgd', short_rounded, compact_value)
        return (mixed / row_total[..., None]).reshape(rows_per_block, QUERY_HEAD_COUNT * HEAD_SIZE).astype(jnp.bfloat16)
    starts = jnp.arange(0, TOKEN_COUNT, rows_per_block, dtype=jnp.int32)
    return lax.map(attend_rows, starts).reshape(TOKEN_COUNT, QUERY_HEAD_COUNT * HEAD_SIZE)
```

```python
import math

import jax
import jax.numpy as jnp
from jax import lax
from jax.experimental import pallas as pl
from jax.experimental.pallas import tpu as pltpu
from jax.sharding import Mesh
from jax.sharding import PartitionSpec as P

HEAD = 128
GROUP = 4
SPAN = 56
PADDED = 64
ROWS = GROUP * SPAN
EXTRA = 16
BATCH = 4
NEG = -1e30
LOG2E = math.log2(math.e)
SCORE_SCALE = LOG2E / math.sqrt(HEAD)
SUMMARY_BIAS = math.log2(SPAN)

ROW = ("xhi", "core", "xlo")
ALL = ROW + ("z", "y")


def nt_dot(a, b):
    return lax.dot_general(a, b, (((1,), (1,)), ((), ())), preferred_element_type=jnp.float32)


def attend_kernel(list_ref, count_ref, own_ref, q_ref, kv_ref, bias_ref, out_ref, padded, sums, base, held):
    key_spans = kv_ref.shape[0]
    query_spans = q_ref.shape[0]
    gap = jnp.zeros((PADDED - SPAN, 2 * HEAD), jnp.bfloat16)

    def prepare(j, carry):
        block = kv_ref[j]
        padded[j] = jnp.concatenate([block, gap], axis=0)
        sums[pl.ds(j, 1), :] = jnp.sum(block.astype(jnp.float32), axis=0, keepdims=True)
        return carry

    lax.fori_loop(0, key_spans, prepare, 0)
    summary = (sums[...] / math.sqrt(SPAN)).astype(jnp.bfloat16)
    summary_keys = summary[:, :HEAD]
    summary_values = summary[:, HEAD:]

    base_cols = key_spans + PADDED
    row = lax.broadcasted_iota(jnp.int32, (ROWS, base_cols), 0) % SPAN
    col = lax.broadcasted_iota(jnp.int32, (ROWS, base_cols), 1) - key_spans
    causal = jnp.where((col >= 0) & (col <= row), 0.0, NEG)
    base_col = lax.broadcasted_iota(jnp.int32, (1, base_cols), 1)
    batch_col = lax.broadcasted_iota(jnp.int32, (1, BATCH * PADDED), 1)
    in_span = batch_col % PADDED < SPAN
    batch_slot = batch_col // PADDED
    pick = (
        lax.broadcasted_iota(jnp.int32, (8, HEAD), 0) == lax.broadcasted_iota(jnp.int32, (8, HEAD), 1)
    ).astype(jnp.bfloat16)
    lane = lax.broadcasted_iota(jnp.int32, (ROWS, HEAD), 1)

    def fold(x):
        return [x[:, k * HEAD : (k + 1) * HEAD] for k in range(x.shape[1] // HEAD)]

    def one_span(s, carry):
        count = count_ref[s]
        own = own_ref[s]
        batches = (count + BATCH - 1) // BATCH
        q = q_ref[s]
        own_block = padded[jnp.maximum(own, 0)]
        base_keys = jnp.concatenate([summary_keys, own_block[:, :HEAD]], axis=0)
        base_values = jnp.concatenate([summary_values, own_block[:, HEAD:]], axis=0)
        own_bias = jnp.where(own >= 0, 0.0, NEG)
        row_bias = jnp.where(base_col < key_spans, bias_ref[pl.ds(s, 1), :], own_bias)
        scores = nt_dot(q, base_keys) * SCORE_SCALE + jnp.where(base_col < key_spans, 0.0, causal) + row_bias
        base[...] = scores
        peak = fold(scores)
        peak = jnp.max(jnp.stack(peak), axis=0) if len(peak) > 1 else peak[0]

        def slots(t):
            blocks = [padded[list_ref[s, t * BATCH + k]] for k in range(BATCH)]
            return jnp.concatenate(blocks, axis=0)

        def score(t, peak):
            keys = slots(t)[:, :HEAD]
            ok = in_span & (batch_slot < count - t * BATCH)
            scores = nt_dot(q, keys) * SCORE_SCALE + jnp.where(ok, 0.0, NEG)
            held[t] = scores
            for part in fold(scores):
                peak = jnp.maximum(peak, part)
            return peak

        peak = lax.fori_loop(0, batches, score, peak)
        peak = jnp.max(peak, axis=1, keepdims=True)

        weight = jnp.exp2(base[...] - peak)
        total = sum(fold(weight))
        mixed = jnp.dot(weight.astype(jnp.bfloat16), base_values, preferred_element_type=jnp.float32)

        def mix(t, state):
            total, mixed = state
            weight = jnp.exp2(held[t] - peak)
            for part in fold(weight):
                total = total + part
            mixed = mixed + jnp.dot(
                weight.astype(jnp.bfloat16), slots(t)[:, HEAD:], preferred_element_type=jnp.float32
            )
            return total, mixed

        total, mixed = lax.fori_loop(0, batches, mix, (total, mixed))
        total = jnp.sum(total, axis=1, keepdims=True)
        out_ref[s, :ROWS, :] = (mixed / total).astype(jnp.bfloat16)
        level = peak + jnp.log2(total)
        high = level.astype(jnp.bfloat16).astype(jnp.float32)
        middle = (level - high).astype(jnp.bfloat16).astype(jnp.float32)
        low = level - high - middle
        parts = jnp.where(lane == 0, high, jnp.where(lane == 1, middle, jnp.where(lane == 2, low, 0.0)))
        flat = nt_dot(pick, parts.astype(jnp.bfloat16))
        tail = jnp.concatenate([flat[:, HEAD:], jnp.zeros((8, 2 * HEAD - ROWS), jnp.float32)], axis=1)
        out_ref[s, ROWS:, :] = jnp.concatenate([flat[:, :HEAD], tail], axis=0).astype(jnp.bfloat16)
        return carry

    lax.fori_loop(0, query_spans, one_span, 0)


def attend(lists, counts, owns, q, kv, bias):
    query_spans, key_spans = q.shape[0], kv.shape[0]
    vmem = pl.BlockSpec(memory_space=pltpu.VMEM)
    smem = pl.BlockSpec(memory_space=pltpu.SMEM)
    return pl.pallas_call(
        attend_kernel,
        out_shape=jax.ShapeDtypeStruct((query_spans, ROWS + EXTRA, HEAD), jnp.bfloat16),
        in_specs=[smem, smem, smem, vmem, vmem, vmem],
        out_specs=vmem,
        scratch_shapes=[
            pltpu.VMEM((key_spans, PADDED, 2 * HEAD), jnp.bfloat16),
            pltpu.VMEM((key_spans, 2 * HEAD), jnp.float32),
            pltpu.VMEM((ROWS, key_spans + PADDED), jnp.float32),
            pltpu.VMEM((key_spans // BATCH, ROWS, BATCH * PADDED), jnp.float32),
        ],
        compiler_params=pltpu.CompilerParams(vmem_limit_bytes=40 * 1024 * 1024),
    )(lists, counts, owns, q, kv, bias)


def combine_kernel(parts_ref, out_ref, *, pieces):
    heads = parts_ref.shape[0] // pieces
    three = (lax.broadcasted_iota(jnp.int32, (8, HEAD), 0) < 3).astype(jnp.bfloat16)

    def spread(rows):
        return lax.dot_general(rows, three, (((0,), (0,)), ((), ())), preferred_element_type=jnp.float32)

    for h in range(heads):
        levels = []
        for y in range(pieces):
            tail = parts_ref[h * pieces + y, ROWS:, :].astype(jnp.float32)
            both = [spread(tail[k * 8 : k * 8 + 8].astype(jnp.bfloat16)) for k in range(2)]
            levels.append(jnp.concatenate(both, axis=0)[:ROWS])
        peak = levels[0]
        for level in levels[1:]:
            peak = jnp.maximum(peak, level)
        total = jnp.zeros_like(peak)
        mixed = jnp.zeros_like(peak)
        for y in range(pieces):
            weight = jnp.exp2(levels[y] - peak)
            total = total + weight
            mixed = mixed + weight * parts_ref[h * pieces + y, :ROWS, :].astype(jnp.float32)
        mixed = (mixed / total)
        for g in range(GROUP):
            at = (h * GROUP + g) * HEAD
            out_ref[:, at : at + HEAD] = mixed[g * SPAN : (g + 1) * SPAN].astype(jnp.bfloat16)


def combine(parts, pieces):
    heads = parts.shape[0] // pieces
    vmem = pl.BlockSpec(memory_space=pltpu.VMEM)

    def kernel(parts_ref, out_ref):
        combine_kernel(parts_ref, out_ref, pieces=pieces)

    return pl.pallas_call(
        kernel,
        out_shape=jax.ShapeDtypeStruct((SPAN, heads * GROUP * HEAD), jnp.bfloat16),
        in_specs=[vmem],
        out_specs=vmem,
        compiler_params=pltpu.CompilerParams(vmem_limit_bytes=32 * 1024 * 1024),
    )(parts)


def tables(query_true, key_true, block_pattern, summary_flag):
    spans = block_pattern.shape[0]
    ids = jnp.arange(spans, dtype=jnp.int32)
    query_pick = (query_true[:, None] == ids[None, :]).astype(jnp.bfloat16)
    key_pick = (key_true[:, None] == ids[None, :]).astype(jnp.bfloat16)
    rows = jnp.dot(query_pick, block_pattern.astype(jnp.bfloat16), preferred_element_type=jnp.float32)
    pattern = nt_dot(rows.astype(jnp.bfloat16), key_pick) > 0.5
    flag = nt_dot((summary_flag == 1).astype(jnp.bfloat16)[None, :], key_pick) > 0.5
    earlier = key_true[None, :] < query_true[:, None]
    full = earlier & pattern
    bias = jnp.where(earlier & ~pattern & flag, SUMMARY_BIAS, NEG).astype(jnp.float32)
    slot = jnp.arange(key_true.shape[0], dtype=jnp.int32)
    upto = (slot[:, None] <= slot[None, :]).astype(jnp.bfloat16)
    rank = jnp.dot(full.astype(jnp.bfloat16), upto, preferred_element_type=jnp.float32).astype(jnp.int32) - 1
    hit = full[:, None, :] & (rank[:, None, :] == slot[None, :, None])
    lists = jnp.sum(jnp.where(hit, slot[None, None, :], 0), axis=2, dtype=jnp.int32)
    counts = jnp.sum(full.astype(jnp.int32), axis=1, dtype=jnp.int32)
    same = key_true[None, :] == query_true[:, None]
    owns = jnp.sum(jnp.where(same, slot[None, :] + 1, 0), axis=1, dtype=jnp.int32) - 1
    bias = jnp.concatenate([bias, jnp.full((bias.shape[0], PADDED), NEG, jnp.float32)], axis=1)
    return lists, counts, owns, bias


def per_device(queries, keys, values, span_order, block_pattern, summary_flag):
    heads = keys.shape[1] // HEAD
    pieces = lax.axis_size("y")
    by_head = [x.reshape(SPAN, heads, HEAD).transpose(1, 0, 2) for x in (keys, values)]
    kv = jnp.concatenate(by_head, axis=2)
    kv = lax.all_to_all(kv, ROW, split_axis=0, concat_axis=0, tiled=True)
    kv = lax.all_gather(kv, "z", axis=0, tiled=True)

    q = queries.reshape(SPAN, heads, GROUP, HEAD).transpose(1, 2, 0, 3).reshape(heads, 1, ROWS, HEAD)
    q = jnp.broadcast_to(q, (heads, pieces, ROWS, HEAD)).reshape(heads * pieces, ROWS, HEAD)
    q = lax.all_to_all(q, ROW + ("y",), split_axis=0, concat_axis=0, tiled=True)

    order = span_order.reshape(heads, lax.axis_size("z"), pieces)
    query_true = lax.dynamic_index_in_dim(order, lax.axis_index("z"), 1, keepdims=False).reshape(-1)
    key_true = lax.dynamic_index_in_dim(order, lax.axis_index("y"), 2, keepdims=False).T.reshape(-1)
    lists, counts, owns, bias = tables(query_true, key_true, block_pattern, summary_flag)
    parts = attend(lists, counts, owns, q, kv, bias)
    parts = lax.all_to_all(parts, ROW + ("y",), split_axis=0, concat_axis=0, tiled=True)
    return combine(parts, pieces)


def solution(mesh):
    fine = Mesh(mesh.devices.reshape(2, 2, 2, 8, 4), ALL)
    return jax.shard_map(
        per_device,
        mesh=fine,
        in_specs=(P(ALL, None), P(ALL, None), P(ALL, None), P(), P(), P()),
        out_specs=P(ALL, None),
        check_vma=False,
    )
```

```python
import math

import jax
import jax.numpy as jnp
from jax import lax
from jax.experimental import pallas as pl
from jax.experimental.pallas import tpu as pltpu
from jax.sharding import Mesh
from jax.sharding import PartitionSpec as P

HEAD = 128
GROUP = 4
SPAN = 56
PADDED = 64
ROWS = GROUP * SPAN
EXTRA = 16
BATCH = 4
TOGETHER = 2
NEG = -1e30
LOG2E = math.log2(math.e)
SCORE_SCALE = LOG2E / math.sqrt(HEAD)
SUMMARY_BIAS = math.log2(SPAN)

HEADS = ("xhi", "xlo", "ylo")
ALL = ("xhi", "core", "xlo", "z", "yhi", "ylo")


def nt_dot(a, b):
    return lax.dot_general(a, b, (((1,), (1,)), ((), ())), preferred_element_type=jnp.float32)


def attend_kernel(
    list_ref, count_ref, own_ref, turn_ref, q_ref, kv_ref, bias_ref, out_ref, sums, base, held, *, together
):
    key_spans = kv_ref.shape[0]
    query_spans = q_ref.shape[0]

    def prepare(j, carry):
        sums[pl.ds(j, 1), :] = jnp.sum(kv_ref[j].astype(jnp.float32), axis=0, keepdims=True)
        return carry

    lax.fori_loop(0, key_spans, prepare, 0, unroll=8)
    summary = (sums[...] / math.sqrt(SPAN)).astype(jnp.bfloat16)

    gap = jnp.zeros((PADDED - SPAN, HEAD), jnp.bfloat16)
    blank = jnp.zeros((PADDED - SPAN, ROWS), jnp.float32)
    key = lax.broadcasted_iota(jnp.int32, (SPAN, ROWS), 0)
    query = lax.broadcasted_iota(jnp.int32, (SPAN, ROWS), 1) % SPAN
    causal = jnp.where(key <= query, 0.0, NEG)
    eye = (
        lax.broadcasted_iota(jnp.int32, (ROWS, ROWS), 0) == lax.broadcasted_iota(jnp.int32, (ROWS, ROWS), 1)
    ).astype(jnp.bfloat16)

    def pile(slots, lanes):
        blocks = []
        for slot in slots:
            blocks += [kv_ref[slot, :, lanes], gap]
        return jnp.concatenate(blocks, axis=0)

    def high(x):
        return jnp.max(x, axis=0, keepdims=True)

    def mixed_by(values, weight):
        return lax.dot_general(
            values, weight.astype(jnp.bfloat16), (((0,), (0,)), ((), ())), preferred_element_type=jnp.float32
        )

    key_lanes, value_lanes = pl.ds(0, HEAD), pl.ds(HEAD, HEAD)

    def some_spans(i, carry):
        spans = [turn_ref[i * together + u] for u in range(together)]
        counts = [count_ref[s] for s in spans]
        owns = [own_ref[s] for s in spans]
        most = counts[0]
        for c in counts[1:]:
            most = jnp.maximum(most, c)
        batches = (most + BATCH - 1) // BATCH

        peaks = []
        for u, s in enumerate(spans):
            keys = jnp.concatenate([summary[:, :HEAD], pile([jnp.maximum(owns[u], 0)], key_lanes)], axis=0)
            scores = nt_dot(keys, q_ref[s]) * SCORE_SCALE
            bias = bias_ref[s]
            far = scores[:key_spans] + jnp.concatenate([bias, bias[:, : ROWS - HEAD]], axis=1)
            near = scores[key_spans : key_spans + SPAN] + (causal + jnp.where(owns[u] >= 0, 0.0, NEG))
            base[u, :key_spans] = far
            base[u, key_spans:] = near
            peaks.append(jnp.maximum(high(far), high(near)))

        def score(t, peaks):
            new = []
            for u, s in enumerate(spans):
                keys = pile([list_ref[s, t * BATCH + k] for k in range(BATCH)], key_lanes)
                scores = nt_dot(keys, q_ref[s]) * SCORE_SCALE
                peak = peaks[u]
                for k in range(BATCH):
                    part = scores[k * PADDED : k * PADDED + SPAN]
                    part = part + jnp.where(t * BATCH + k < counts[u], 0.0, NEG)
                    held[u, t, k * SPAN : (k + 1) * SPAN] = part
                    peak = jnp.maximum(peak, high(part))
                new.append(peak)
            return tuple(new)

        peaks = lax.fori_loop(0, batches, score, tuple(peaks))

        state = []
        for u, s in enumerate(spans):
            weight = jnp.exp2(base[u] - peaks[u])
            values = jnp.concatenate([summary[:, HEAD:], pile([jnp.maximum(owns[u], 0)], value_lanes)], axis=0)
            total = jnp.sum(weight, axis=0, keepdims=True)
            state.append((total, mixed_by(values, jnp.concatenate([weight, blank], axis=0))))

        def mix(t, state):
            new = []
            for u, s in enumerate(spans):
                total, mixed = state[u]
                values = pile([list_ref[s, t * BATCH + k] for k in range(BATCH)], value_lanes)
                weight = jnp.exp2(held[u, t] - peaks[u])
                total = total + jnp.sum(weight, axis=0, keepdims=True)
                parts = []
                for k in range(BATCH):
                    parts += [weight[k * SPAN : (k + 1) * SPAN], blank]
                new.append((total, mixed + mixed_by(values, jnp.concatenate(parts, axis=0))))
            return tuple(new)

        state = lax.fori_loop(0, batches, mix, tuple(state))
        for u, s in enumerate(spans):
            total, mixed = state[u]
            out_ref[s, :ROWS, :] = nt_dot(eye, (mixed / total).astype(jnp.bfloat16)).astype(jnp.bfloat16)
            level = peaks[u] + jnp.log2(total)
            first = level.astype(jnp.bfloat16).astype(jnp.float32)
            second = (level - first).astype(jnp.bfloat16).astype(jnp.float32)
            rows = jnp.concatenate([first, second, level - first - second, blank[:5]], axis=0)
            rows = jnp.concatenate([rows, jnp.zeros((8, 2 * HEAD - ROWS), jnp.float32)], axis=1)
            rows = jnp.concatenate([rows[:, :HEAD], rows[:, HEAD:]], axis=0)
            out_ref[s, ROWS:, :] = rows.astype(jnp.bfloat16)
        return carry

    lax.fori_loop(0, query_spans // together, some_spans, 0)


def attend(lists, counts, owns, turns, q, kv, bias):
    query_spans, key_spans = q.shape[0], kv.shape[0]
    vmem = pl.BlockSpec(memory_space=pltpu.VMEM)
    smem = pl.BlockSpec(memory_space=pltpu.SMEM)

    def kernel(*refs):
        attend_kernel(*refs, together=TOGETHER)

    return pl.pallas_call(
        kernel,
        out_shape=jax.ShapeDtypeStruct((query_spans, ROWS + EXTRA, HEAD), jnp.bfloat16),
        in_specs=[smem, smem, smem, smem, vmem, vmem, vmem],
        out_specs=vmem,
        scratch_shapes=[
            pltpu.VMEM((key_spans, 2 * HEAD), jnp.float32),
            pltpu.VMEM((TOGETHER, key_spans + SPAN, ROWS), jnp.float32),
            pltpu.VMEM((TOGETHER, key_spans // BATCH, BATCH * SPAN, ROWS), jnp.float32),
        ],
        compiler_params=pltpu.CompilerParams(vmem_limit_bytes=48 * 1024 * 1024),
    )(lists, counts, owns, turns, q, kv, bias)


def combine_kernel(parts_ref, out_ref, *, pieces):
    heads = parts_ref.shape[0] // pieces
    three = (lax.broadcasted_iota(jnp.int32, (8, HEAD), 0) < 3).astype(jnp.bfloat16)

    def spread(rows):
        return lax.dot_general(rows, three, (((0,), (0,)), ((), ())), preferred_element_type=jnp.float32)

    for h in range(heads):
        levels = []
        for y in range(pieces):
            tail = parts_ref[h * pieces + y, ROWS:, :].astype(jnp.float32)
            both = [spread(tail[k * 8 : k * 8 + 8].astype(jnp.bfloat16)) for k in range(2)]
            levels.append(jnp.concatenate(both, axis=0)[:ROWS])
        peak = levels[0]
        for level in levels[1:]:
            peak = jnp.maximum(peak, level)
        total = jnp.zeros_like(peak)
        mixed = jnp.zeros_like(peak)
        for y in range(pieces):
            weight = jnp.exp2(levels[y] - peak)
            total = total + weight
            mixed = mixed + weight * parts_ref[h * pieces + y, :ROWS, :].astype(jnp.float32)
        mixed = (mixed / total)
        for g in range(GROUP):
            at = (h * GROUP + g) * HEAD
            out_ref[:, at : at + HEAD] = mixed[g * SPAN : (g + 1) * SPAN].astype(jnp.bfloat16)


def combine(parts, pieces):
    heads = parts.shape[0] // pieces
    vmem = pl.BlockSpec(memory_space=pltpu.VMEM)

    def kernel(parts_ref, out_ref):
        combine_kernel(parts_ref, out_ref, pieces=pieces)

    return pl.pallas_call(
        kernel,
        out_shape=jax.ShapeDtypeStruct((SPAN, heads * GROUP * HEAD), jnp.bfloat16),
        in_specs=[vmem],
        out_specs=vmem,
        compiler_params=pltpu.CompilerParams(vmem_limit_bytes=32 * 1024 * 1024),
    )(parts)


def tables(query_true, key_true, block_pattern, summary_flag):
    spans = block_pattern.shape[0]
    ids = jnp.arange(spans, dtype=jnp.int32)
    query_pick = (query_true[:, None] == ids[None, :]).astype(jnp.bfloat16)
    key_pick = (key_true[:, None] == ids[None, :]).astype(jnp.bfloat16)
    rows = jnp.dot(query_pick, block_pattern.astype(jnp.bfloat16), preferred_element_type=jnp.float32)
    pattern = nt_dot(rows.astype(jnp.bfloat16), key_pick) > 0.5
    flag = nt_dot((summary_flag == 1).astype(jnp.bfloat16)[None, :], key_pick) > 0.5
    earlier = key_true[None, :] < query_true[:, None]
    full = earlier & pattern
    bias = jnp.where(earlier & ~pattern & flag, SUMMARY_BIAS, NEG).astype(jnp.float32)
    slot = jnp.arange(key_true.shape[0], dtype=jnp.int32)
    upto = (slot[:, None] <= slot[None, :]).astype(jnp.bfloat16)
    rank = jnp.dot(full.astype(jnp.bfloat16), upto, preferred_element_type=jnp.float32).astype(jnp.int32) - 1
    hit = full[:, None, :] & (rank[:, None, :] == slot[None, :, None])
    lists = jnp.sum(jnp.where(hit, slot[None, None, :], 0), axis=2, dtype=jnp.int32)
    counts = jnp.sum(full.astype(jnp.int32), axis=1, dtype=jnp.int32)
    same = key_true[None, :] == query_true[:, None]
    owns = jnp.sum(jnp.where(same, slot[None, :] + 1, 0), axis=1, dtype=jnp.int32) - 1
    bias = jnp.broadcast_to(bias[:, :, None], bias.shape + (HEAD,))
    ids = jnp.arange(counts.shape[0], dtype=jnp.int32)
    ahead = (counts[None, :] > counts[:, None]) | ((counts[None, :] == counts[:, None]) & (ids[None, :] < ids[:, None]))
    place = jnp.sum(ahead.astype(jnp.int32), axis=1, dtype=jnp.int32)
    turns = jnp.sum(jnp.where(place[None, :] == ids[:, None], ids[None, :], 0), axis=1, dtype=jnp.int32)
    return lists, counts, owns, turns, bias


def per_device(queries, keys, values, span_order, block_pattern, summary_flag):
    heads = keys.shape[1] // HEAD
    pieces = lax.axis_size("yhi")
    by_head = [x.reshape(SPAN, heads, HEAD).transpose(1, 0, 2) for x in (keys, values)]
    kv = jnp.concatenate(by_head, axis=2)
    kv = lax.all_to_all(kv, HEADS, split_axis=0, concat_axis=0, tiled=True)
    kv = lax.all_gather(kv, ("z", "core"), axis=0, tiled=True)

    order = span_order.reshape(2, 2, 2, lax.axis_size("z"), 2, 2)
    query_true = lax.dynamic_index_in_dim(order, lax.axis_index("z"), 3, keepdims=False)
    query_true = lax.dynamic_index_in_dim(query_true, lax.axis_index("core"), 1, keepdims=False)
    query_true = query_true.transpose(0, 1, 3, 2).reshape(-1)
    key_true = lax.dynamic_index_in_dim(order, lax.axis_index("yhi"), 4, keepdims=False)
    key_true = key_true.transpose(3, 1, 0, 2, 4).reshape(-1)

    q = queries.reshape(SPAN, heads, GROUP, HEAD).transpose(1, 2, 0, 3).reshape(heads, 1, ROWS, HEAD)
    q = jnp.broadcast_to(q, (heads, pieces, ROWS, HEAD)).reshape(heads * pieces, ROWS, HEAD)
    q = lax.all_to_all(q, HEADS + ("yhi",), split_axis=0, concat_axis=0, tiled=True)

    lists, counts, owns, turns, bias = tables(query_true, key_true, block_pattern, summary_flag)
    parts = attend(lists, counts, owns, turns, q, kv, bias)
    parts = lax.all_to_all(parts, HEADS + ("yhi",), split_axis=0, concat_axis=0, tiled=True)
    return combine(parts, pieces)


def solution(mesh):
    fine = Mesh(mesh.devices.reshape(2, 2, 2, 8, 2, 2), ALL)
    return jax.shard_map(
        per_device,
        mesh=fine,
        in_specs=(P(ALL, None), P(ALL, None), P(ALL, None), P(), P(), P()),
        out_specs=P(ALL, None),
        check_vma=False,
    )
```

```python
import math

import jax
import jax.numpy as jnp
from jax import lax
from jax.experimental import pallas as pl
from jax.experimental.pallas import tpu as pltpu
from jax.sharding import Mesh
from jax.sharding import PartitionSpec as P

HEAD = 128
GROUP = 4
SPAN = 56
PADDED = 64
ROWS = GROUP * SPAN
EXTRA = 16
BATCH = 4
TOGETHER = 4
NEG = -1e30
LOG2E = math.log2(math.e)
SCORE_SCALE = LOG2E / math.sqrt(HEAD)
SUMMARY_BIAS = math.log2(SPAN)

HEADS = ("xhi", "xlo", "ylo")
ALL = ("xhi", "core", "xlo", "z", "yhi", "ylo")


def nt_dot(a, b):
    return lax.dot_general(a, b, (((1,), (1,)), ((), ())), preferred_element_type=jnp.float32)


def attend_kernel(
    list_ref, count_ref, own_ref, turn_ref, q_ref, bias_ref, *refs, pieces, together
):
    piece_refs, (out_ref, kv_ref, sums, base, held, turned) = refs[:pieces], refs[pieces:]
    key_spans = kv_ref.shape[0]
    query_spans = q_ref.shape[0]

    first = 0
    for piece_ref in piece_refs:

        def prepare(j, carry, piece_ref=piece_ref, first=first):
            block = piece_ref[j]
            kv_ref[first + j] = block
            sums[pl.ds(first + j, 1), :] = jnp.sum(block.astype(jnp.float32), axis=0, keepdims=True)
            return carry

        lax.fori_loop(0, piece_ref.shape[0], prepare, 0, unroll=8)
        first += piece_ref.shape[0]
    summary = (sums[...] / math.sqrt(SPAN)).astype(jnp.bfloat16)

    gap = jnp.zeros((PADDED - SPAN, HEAD), jnp.bfloat16)
    blank = jnp.zeros((PADDED - SPAN, ROWS), jnp.float32)
    key = lax.broadcasted_iota(jnp.int32, (SPAN, ROWS), 0)
    query = lax.broadcasted_iota(jnp.int32, (SPAN, ROWS), 1) % SPAN
    causal = jnp.where(key <= query, 0.0, NEG)
    eye = (
        lax.broadcasted_iota(jnp.int32, (ROWS, ROWS), 0) == lax.broadcasted_iota(jnp.int32, (ROWS, ROWS), 1)
    ).astype(jnp.bfloat16)

    def pile(slots, lanes):
        blocks = []
        for slot in slots:
            blocks += [kv_ref[slot, :, lanes], gap]
        return jnp.concatenate(blocks, axis=0)

    def high(x):
        return jnp.max(x.reshape(x.shape[0] // 8, 8, x.shape[1]), axis=0)

    def add(x):
        return jnp.sum(x.reshape(x.shape[0] // 8, 8, x.shape[1]), axis=0)

    def mixed_by(values, weight):
        return lax.dot_general(
            values, weight.astype(jnp.bfloat16), (((0,), (0,)), ((), ())), preferred_element_type=jnp.float32
        )

    key_lanes, value_lanes = pl.ds(0, HEAD), pl.ds(HEAD, HEAD)

    def some_spans(i, carry):
        spans = [turn_ref[i * together + u] for u in range(together)]
        counts = [count_ref[s] for s in spans]
        owns = [own_ref[s] for s in spans]
        most = counts[0]
        for c in counts[1:]:
            most = jnp.maximum(most, c)
        batches = (most + BATCH - 1) // BATCH

        for u, s in enumerate(spans):
            turned[u] = q_ref[s].T

        peaks = []
        for u, s in enumerate(spans):
            keys = jnp.concatenate([summary[:, :HEAD], pile([jnp.maximum(owns[u], 0)], key_lanes)], axis=0)
            scores = jnp.dot(keys, turned[u], preferred_element_type=jnp.float32) * SCORE_SCALE
            here = (lax.broadcasted_iota(jnp.int32, (bias_ref.shape[1], ROWS), 0) == s).astype(jnp.bfloat16)
            far = scores[:key_spans] + SUMMARY_BIAS + jnp.dot(bias_ref[...], here, preferred_element_type=jnp.float32)
            near = scores[key_spans : key_spans + SPAN] + (causal + jnp.where(owns[u] >= 0, 0.0, NEG))
            base[u, :key_spans] = far
            base[u, key_spans:] = near
            peaks.append(jnp.maximum(high(far), high(near)))

        def score(t, peaks):
            new = []
            for u, s in enumerate(spans):
                keys = pile([list_ref[s, t * BATCH + k] for k in range(BATCH)], key_lanes)
                scores = jnp.dot(keys, turned[u], preferred_element_type=jnp.float32) * SCORE_SCALE
                peak = peaks[u]
                for k in range(BATCH):
                    part = scores[k * PADDED : k * PADDED + SPAN]
                    part = part + jnp.where(t * BATCH + k < counts[u], 0.0, NEG)
                    held[u, t, k * SPAN : (k + 1) * SPAN] = part
                    peak = jnp.maximum(peak, high(part))
                new.append(peak)
            return tuple(new)

        peaks = lax.fori_loop(0, batches, score, tuple(peaks))
        peaks = [jnp.max(peak, axis=0, keepdims=True) for peak in peaks]

        state = []
        for u, s in enumerate(spans):
            weight = jnp.exp2(base[u] - peaks[u])
            values = jnp.concatenate([summary[:, HEAD:], pile([jnp.maximum(owns[u], 0)], value_lanes)], axis=0)
            total = add(weight)
            state.append((total, mixed_by(values, jnp.concatenate([weight, blank], axis=0))))

        def mix(t, state):
            new = []
            for u, s in enumerate(spans):
                total, mixed = state[u]
                values = pile([list_ref[s, t * BATCH + k] for k in range(BATCH)], value_lanes)
                weight = jnp.exp2(held[u, t] - peaks[u])
                total = total + add(weight)
                parts = []
                for k in range(BATCH):
                    parts += [weight[k * SPAN : (k + 1) * SPAN], blank]
                new.append((total, mixed + mixed_by(values, jnp.concatenate(parts, axis=0))))
            return tuple(new)

        state = lax.fori_loop(0, batches, mix, tuple(state))
        for u, s in enumerate(spans):
            total, mixed = state[u]
            total = jnp.sum(total, axis=0, keepdims=True)
            out_ref[s, :ROWS, :] = nt_dot(eye, (mixed / total).astype(jnp.bfloat16)).astype(jnp.bfloat16)
            level = peaks[u] + jnp.log2(total)
            first = level.astype(jnp.bfloat16).astype(jnp.float32)
            second = (level - first).astype(jnp.bfloat16).astype(jnp.float32)
            rows = jnp.concatenate([first, second, level - first - second, blank[:5]], axis=0)
            rows = jnp.concatenate([rows, jnp.zeros((8, 2 * HEAD - ROWS), jnp.float32)], axis=1)
            rows = jnp.concatenate([rows[:, :HEAD], rows[:, HEAD:]], axis=0)
            out_ref[s, ROWS:, :] = rows.astype(jnp.bfloat16)
        return carry

    lax.fori_loop(0, query_spans // together, some_spans, 0)


def attend(lists, counts, owns, turns, q, pieces, bias):
    query_spans, key_spans = q.shape[0], sum(piece.shape[0] for piece in pieces)
    vmem = pl.BlockSpec(memory_space=pltpu.VMEM)
    smem = pl.BlockSpec(memory_space=pltpu.SMEM)

    def kernel(*refs):
        attend_kernel(*refs, pieces=len(pieces), together=TOGETHER)

    return pl.pallas_call(
        kernel,
        out_shape=jax.ShapeDtypeStruct((query_spans, ROWS + EXTRA, HEAD), jnp.bfloat16),
        in_specs=[smem] * 4 + [vmem] * (2 + len(pieces)),
        out_specs=vmem,
        scratch_shapes=[
            pltpu.VMEM((key_spans, SPAN, 2 * HEAD), jnp.bfloat16),
            pltpu.VMEM((key_spans, 2 * HEAD), jnp.float32),
            pltpu.VMEM((TOGETHER, key_spans + SPAN, ROWS), jnp.float32),
            pltpu.VMEM((TOGETHER, key_spans // BATCH, BATCH * SPAN, ROWS), jnp.float32),
            pltpu.VMEM((TOGETHER, HEAD, ROWS), jnp.bfloat16),
        ],
        compiler_params=pltpu.CompilerParams(vmem_limit_bytes=48 * 1024 * 1024),
    )(lists, counts, owns, turns, q, bias, *pieces)


def combine_kernel(parts_ref, out_ref, *, pieces):
    heads = parts_ref.shape[0] // pieces
    three = (lax.broadcasted_iota(jnp.int32, (8, HEAD), 0) < 3).astype(jnp.bfloat16)

    def spread(rows):
        return lax.dot_general(rows, three, (((0,), (0,)), ((), ())), preferred_element_type=jnp.float32)

    for h in range(heads):
        levels = []
        for y in range(pieces):
            tail = parts_ref[h * pieces + y, ROWS:, :].astype(jnp.float32)
            both = [spread(tail[k * 8 : k * 8 + 8].astype(jnp.bfloat16)) for k in range(2)]
            levels.append(jnp.concatenate(both, axis=0)[:ROWS])
        peak = levels[0]
        for level in levels[1:]:
            peak = jnp.maximum(peak, level)
        total = jnp.zeros_like(peak)
        mixed = jnp.zeros_like(peak)
        for y in range(pieces):
            weight = jnp.exp2(levels[y] - peak)
            total = total + weight
            mixed = mixed + weight * parts_ref[h * pieces + y, :ROWS, :].astype(jnp.float32)
        mixed = (mixed / total)
        for g in range(GROUP):
            at = (h * GROUP + g) * HEAD
            out_ref[:, at : at + HEAD] = mixed[g * SPAN : (g + 1) * SPAN].astype(jnp.bfloat16)


def combine(parts, pieces):
    heads = parts.shape[0] // pieces
    vmem = pl.BlockSpec(memory_space=pltpu.VMEM)

    def kernel(parts_ref, out_ref):
        combine_kernel(parts_ref, out_ref, pieces=pieces)

    return pl.pallas_call(
        kernel,
        out_shape=jax.ShapeDtypeStruct((SPAN, heads * GROUP * HEAD), jnp.bfloat16),
        in_specs=[vmem],
        out_specs=vmem,
        compiler_params=pltpu.CompilerParams(vmem_limit_bytes=32 * 1024 * 1024),
    )(parts)


def tables(query_true, key_true, block_pattern, summary_flag):
    spans = block_pattern.shape[0]
    ids = jnp.arange(spans, dtype=jnp.int32)
    query_pick = (query_true[:, None] == ids[None, :]).astype(jnp.bfloat16)
    key_pick = (key_true[:, None] == ids[None, :]).astype(jnp.bfloat16)
    rows = jnp.dot(query_pick, block_pattern.astype(jnp.bfloat16), preferred_element_type=jnp.float32)
    pattern = nt_dot(rows.astype(jnp.bfloat16), key_pick) > 0.5
    flag = nt_dot((summary_flag == 1).astype(jnp.bfloat16)[None, :], key_pick) > 0.5
    earlier = key_true[None, :] < query_true[:, None]
    full = earlier & pattern
    bias = jnp.where(earlier & ~pattern & flag, 0.0, NEG).T.astype(jnp.bfloat16)
    slot = jnp.arange(key_true.shape[0], dtype=jnp.int32)
    upto = (slot[:, None] <= slot[None, :]).astype(jnp.bfloat16)
    rank = jnp.dot(full.astype(jnp.bfloat16), upto, preferred_element_type=jnp.float32).astype(jnp.int32) - 1
    hit = full[:, None, :] & (rank[:, None, :] == slot[None, :, None])
    lists = jnp.sum(jnp.where(hit, slot[None, None, :], 0), axis=2, dtype=jnp.int32)
    counts = jnp.sum(full.astype(jnp.int32), axis=1, dtype=jnp.int32)
    same = key_true[None, :] == query_true[:, None]
    owns = jnp.sum(jnp.where(same, slot[None, :] + 1, 0), axis=1, dtype=jnp.int32) - 1
    ids = jnp.arange(counts.shape[0], dtype=jnp.int32)
    ahead = (counts[None, :] > counts[:, None]) | ((counts[None, :] == counts[:, None]) & (ids[None, :] < ids[:, None]))
    place = jnp.sum(ahead.astype(jnp.int32), axis=1, dtype=jnp.int32)
    turns = jnp.sum(jnp.where(place[None, :] == ids[:, None], ids[None, :], 0), axis=1, dtype=jnp.int32)
    return lists, counts, owns, turns, bias


STEPS = (0, -1, 1, -2, 2, -3, 3, 4)


def shift(x, axis, by):
    n = lax.axis_size(axis)
    return lax.ppermute(x, axis, [(i, (i + by) % n) for i in range(n)])


def ring(kv):
    half = kv.shape[0] // 2
    up, down, held = kv, kv, [kv]
    for _ in range(3):
        up, down = shift(up, "z", 1), shift(down, "z", -1)
        held += [up, down]
    held += [shift(up[:half], "z", 1), shift(down[half:], "z", -1)]
    near, far = jnp.concatenate(held[:5]), jnp.concatenate(held[5:])
    return [near, far, shift(near, "core", 1), shift(far, "core", 1)]


def per_device(queries, keys, values, span_order, block_pattern, summary_flag):
    heads = keys.shape[1] // HEAD
    pieces = lax.axis_size("yhi")
    by_head = [x.reshape(SPAN, heads, HEAD).transpose(1, 0, 2) for x in (keys, values)]
    kv = jnp.concatenate(by_head, axis=2)
    kv = lax.all_to_all(kv, HEADS, split_axis=0, concat_axis=0, tiled=True)
    pieces_of_keys = ring(kv)

    order = span_order.reshape(2, 2, 2, lax.axis_size("z"), 2, 2)
    query_true = lax.dynamic_index_in_dim(order, lax.axis_index("z"), 3, keepdims=False)
    query_true = lax.dynamic_index_in_dim(query_true, lax.axis_index("core"), 1, keepdims=False)
    query_true = query_true.transpose(0, 1, 3, 2).reshape(-1)
    key_true = lax.dynamic_index_in_dim(order, lax.axis_index("yhi"), 4, keepdims=False)
    key_true = key_true.transpose(1, 3, 0, 2, 4)
    core, depth, z = lax.axis_index("core"), lax.axis_size("z"), lax.axis_index("z")
    key_true = jnp.take(key_true, (core + jnp.arange(2, dtype=jnp.int32)) % 2, axis=0)
    key_true = jnp.take(key_true, (z + jnp.array(STEPS, jnp.int32) + depth) % depth, axis=1).reshape(-1)

    q = queries.reshape(SPAN, heads, GROUP, HEAD).transpose(1, 2, 0, 3).reshape(heads, 1, ROWS, HEAD)
    q = jnp.broadcast_to(q, (heads, pieces, ROWS, HEAD)).reshape(heads * pieces, ROWS, HEAD)
    q = lax.all_to_all(q, HEADS + ("yhi",), split_axis=0, concat_axis=0, tiled=True)

    lists, counts, owns, turns, bias = tables(query_true, key_true, block_pattern, summary_flag)
    parts = attend(lists, counts, owns, turns, q, pieces_of_keys, bias)
    parts = lax.all_to_all(parts, HEADS + ("yhi",), split_axis=0, concat_axis=0, tiled=True)
    return combine(parts, pieces)


def solution(mesh):
    fine = Mesh(mesh.devices.reshape(2, 2, 2, 8, 2, 2), ALL)
    return jax.shard_map(
        per_device,
        mesh=fine,
        in_specs=(P(ALL, None), P(ALL, None), P(ALL, None), P(), P(), P()),
        out_specs=P(ALL, None),
        check_vma=False,
    )
```

```python
import math

import jax
import jax.numpy as jnp
from jax import lax
from jax.experimental import pallas as pl
from jax.experimental.pallas import tpu as pltpu
from jax.sharding import Mesh
from jax.sharding import PartitionSpec as P

HEAD = 128
GROUP = 4
SPAN = 56
PADDED = 64
ROWS = GROUP * SPAN
EXTRA = 16
BATCH = 4
TOGETHER = 4
NEG = -1e30
LOG2E = math.log2(math.e)
SCORE_SCALE = LOG2E / math.sqrt(HEAD)
SUMMARY_BIAS = math.log2(SPAN)

HEADS = ("xhi", "xlo", "ylo")
ALL = ("xhi", "core", "xlo", "z", "yhi", "ylo")


def nt_dot(a, b):
    return lax.dot_general(a, b, (((1,), (1,)), ((), ())), preferred_element_type=jnp.float32)


def attend_kernel(
    table_ref, mask_ref, ours_ref, theirs_ref, *refs, pieces, together
):
    piece_refs, (out_ref, kv_ref, sums, base, held, turned) = refs[:pieces], refs[pieces:]
    key_spans = kv_ref.shape[0]
    query_spans = out_ref.shape[0]
    count_at, own_at, turn_at, side_at = range(key_spans, key_spans + 4)
    side = table_ref[0, side_at]

    first = 0
    for piece_ref in piece_refs:

        def prepare(j, carry, piece_ref=piece_ref, first=first):
            block = piece_ref[j]
            kv_ref[first + j] = block
            sums[pl.ds(first + j, 1), :] = jnp.sum(block.astype(jnp.float32), axis=0, keepdims=True)
            return carry

        lax.fori_loop(0, piece_ref.shape[0], prepare, 0, unroll=8)
        first += piece_ref.shape[0]
    summary = (sums[...] / math.sqrt(SPAN)).astype(jnp.bfloat16)

    gap = jnp.zeros((PADDED - SPAN, HEAD), jnp.bfloat16)
    blank = jnp.zeros((PADDED - SPAN, ROWS), jnp.float32)
    key = lax.broadcasted_iota(jnp.int32, (SPAN, ROWS), 0)
    query = lax.broadcasted_iota(jnp.int32, (SPAN, ROWS), 1) % SPAN
    causal = jnp.where(key <= query, 0.0, NEG)
    eye = (
        lax.broadcasted_iota(jnp.int32, (ROWS, ROWS), 0) == lax.broadcasted_iota(jnp.int32, (ROWS, ROWS), 1)
    ).astype(jnp.bfloat16)

    def pile(slots, lanes):
        blocks = []
        for slot in slots:
            blocks += [kv_ref[slot, :, lanes], gap]
        return jnp.concatenate(blocks, axis=0)

    def high(x):
        return jnp.max(x.reshape(x.shape[0] // 8, 8, x.shape[1]), axis=0)

    def add(x):
        return jnp.sum(x.reshape(x.shape[0] // 8, 8, x.shape[1]), axis=0)

    def mixed_by(values, weight):
        return lax.dot_general(
            values, weight.astype(jnp.bfloat16), (((0,), (0,)), ((), ())), preferred_element_type=jnp.float32
        )

    key_lanes, value_lanes = pl.ds(0, HEAD), pl.ds(HEAD, HEAD)

    def some_spans(i, carry):
        spans = [table_ref[i * together + u, turn_at] for u in range(together)]
        counts = [table_ref[s, count_at] for s in spans]
        owns = [table_ref[s, own_at] for s in spans]
        most = counts[0]
        for c in counts[1:]:
            most = jnp.maximum(most, c)
        batches = (most + BATCH - 1) // BATCH

        for u, s in enumerate(spans):
            rows = jnp.where(s % 2 == side, ours_ref[s // 2], theirs_ref[s // 2]).astype(jnp.float32)
            rows = jnp.concatenate([rows[:, g * HEAD : (g + 1) * HEAD] for g in range(GROUP)], axis=0)
            turned[u] = rows.astype(jnp.bfloat16).T

        peaks = []
        for u, s in enumerate(spans):
            keys = jnp.concatenate([summary[:, :HEAD], pile([jnp.maximum(owns[u], 0)], key_lanes)], axis=0)
            scores = jnp.dot(keys, turned[u], preferred_element_type=jnp.float32) * SCORE_SCALE
            here = (lax.broadcasted_iota(jnp.int32, (mask_ref.shape[1], ROWS), 0) == s).astype(jnp.bfloat16)
            far = scores[:key_spans] + SUMMARY_BIAS + jnp.dot(mask_ref[...], here, preferred_element_type=jnp.float32)
            near = scores[key_spans : key_spans + SPAN] + (causal + jnp.where(owns[u] >= 0, 0.0, NEG))
            base[u, :key_spans] = far
            base[u, key_spans:] = near
            peaks.append(jnp.maximum(high(far), high(near)))

        def score(t, peaks):
            new = []
            for u, s in enumerate(spans):
                keys = pile([table_ref[s, t * BATCH + k] for k in range(BATCH)], key_lanes)
                scores = jnp.dot(keys, turned[u], preferred_element_type=jnp.float32) * SCORE_SCALE
                peak = peaks[u]
                for k in range(BATCH):
                    part = scores[k * PADDED : k * PADDED + SPAN]
                    part = part + jnp.where(t * BATCH + k < counts[u], 0.0, NEG)
                    held[u, t, k * SPAN : (k + 1) * SPAN] = part
                    peak = jnp.maximum(peak, high(part))
                new.append(peak)
            return tuple(new)

        peaks = lax.fori_loop(0, batches, score, tuple(peaks))
        peaks = [jnp.max(peak, axis=0, keepdims=True) for peak in peaks]

        state = []
        for u, s in enumerate(spans):
            weight = jnp.exp2(base[u] - peaks[u])
            values = jnp.concatenate([summary[:, HEAD:], pile([jnp.maximum(owns[u], 0)], value_lanes)], axis=0)
            total = add(weight)
            state.append((total, mixed_by(values, jnp.concatenate([weight, blank], axis=0))))

        def mix(t, state):
            new = []
            for u, s in enumerate(spans):
                total, mixed = state[u]
                values = pile([table_ref[s, t * BATCH + k] for k in range(BATCH)], value_lanes)
                weight = jnp.exp2(held[u, t] - peaks[u])
                total = total + add(weight)
                parts = []
                for k in range(BATCH):
                    parts += [weight[k * SPAN : (k + 1) * SPAN], blank]
                new.append((total, mixed + mixed_by(values, jnp.concatenate(parts, axis=0))))
            return tuple(new)

        state = lax.fori_loop(0, batches, mix, tuple(state))
        for u, s in enumerate(spans):
            total, mixed = state[u]
            total = jnp.sum(total, axis=0, keepdims=True)
            out_ref[s, :ROWS, :] = nt_dot(eye, (mixed / total).astype(jnp.bfloat16)).astype(jnp.bfloat16)
            level = peaks[u] + jnp.log2(total)
            first = level.astype(jnp.bfloat16).astype(jnp.float32)
            second = (level - first).astype(jnp.bfloat16).astype(jnp.float32)
            rows = jnp.concatenate([first, second, level - first - second, blank[:5]], axis=0)
            rows = jnp.concatenate([rows, jnp.zeros((8, 2 * HEAD - ROWS), jnp.float32)], axis=1)
            rows = jnp.concatenate([rows[:, :HEAD], rows[:, HEAD:]], axis=0)
            out_ref[s, ROWS:, :] = rows.astype(jnp.bfloat16)
        return carry

    lax.fori_loop(0, query_spans // together, some_spans, 0)


def attend(table, mask, ours, theirs, pieces):
    query_spans, key_spans = table.shape[0], sum(piece.shape[0] for piece in pieces)
    vmem = pl.BlockSpec(memory_space=pltpu.VMEM)
    smem = pl.BlockSpec(memory_space=pltpu.SMEM)

    def kernel(*refs):
        attend_kernel(*refs, pieces=len(pieces), together=TOGETHER)

    return pl.pallas_call(
        kernel,
        out_shape=jax.ShapeDtypeStruct((query_spans, ROWS + EXTRA, HEAD), jnp.bfloat16),
        in_specs=[smem] + [vmem] * (3 + len(pieces)),
        out_specs=vmem,
        scratch_shapes=[
            pltpu.VMEM((key_spans, SPAN, 2 * HEAD), jnp.bfloat16),
            pltpu.VMEM((key_spans, 2 * HEAD), jnp.float32),
            pltpu.VMEM((TOGETHER, key_spans + SPAN, ROWS), jnp.float32),
            pltpu.VMEM((TOGETHER, key_spans // BATCH, BATCH * SPAN, ROWS), jnp.float32),
            pltpu.VMEM((TOGETHER, HEAD, ROWS), jnp.bfloat16),
        ],
        compiler_params=pltpu.CompilerParams(vmem_limit_bytes=48 * 1024 * 1024),
    )(table, mask, ours, theirs, *pieces)


def combine_kernel(parts_ref, out_ref, *, pieces):
    heads = parts_ref.shape[0] // pieces
    three = (lax.broadcasted_iota(jnp.int32, (8, HEAD), 0) < 3).astype(jnp.bfloat16)

    def spread(rows):
        return lax.dot_general(rows, three, (((0,), (0,)), ((), ())), preferred_element_type=jnp.float32)

    for h in range(heads):
        levels = []
        for y in range(pieces):
            tail = parts_ref[h * pieces + y, ROWS:, :].astype(jnp.float32)
            both = [spread(tail[k * 8 : k * 8 + 8].astype(jnp.bfloat16)) for k in range(2)]
            levels.append(jnp.concatenate(both, axis=0)[:ROWS])
        peak = levels[0]
        for level in levels[1:]:
            peak = jnp.maximum(peak, level)
        total = jnp.zeros_like(peak)
        mixed = jnp.zeros_like(peak)
        for y in range(pieces):
            weight = jnp.exp2(levels[y] - peak)
            total = total + weight
            mixed = mixed + weight * parts_ref[h * pieces + y, :ROWS, :].astype(jnp.float32)
        mixed = (mixed / total)
        for g in range(GROUP):
            at = (h * GROUP + g) * HEAD
            out_ref[:, at : at + HEAD] = mixed[g * SPAN : (g + 1) * SPAN].astype(jnp.bfloat16)


def combine(parts, pieces):
    heads = parts.shape[0] // pieces
    vmem = pl.BlockSpec(memory_space=pltpu.VMEM)

    def kernel(parts_ref, out_ref):
        combine_kernel(parts_ref, out_ref, pieces=pieces)

    return pl.pallas_call(
        kernel,
        out_shape=jax.ShapeDtypeStruct((SPAN, heads * GROUP * HEAD), jnp.bfloat16),
        in_specs=[vmem],
        out_specs=vmem,
        compiler_params=pltpu.CompilerParams(vmem_limit_bytes=32 * 1024 * 1024),
    )(parts)


def tables(query_true, key_true, side, block_pattern, summary_flag):
    spans = block_pattern.shape[0]
    ids = jnp.arange(spans, dtype=jnp.int32)
    query_pick = (query_true[:, None] == ids[None, :]).astype(jnp.bfloat16)
    key_pick = (key_true[:, None] == ids[None, :]).astype(jnp.bfloat16)
    rows = jnp.dot(query_pick, block_pattern.astype(jnp.bfloat16), preferred_element_type=jnp.float32)
    pattern = nt_dot(rows.astype(jnp.bfloat16), key_pick) > 0.5
    flag = nt_dot((summary_flag == 1).astype(jnp.bfloat16)[None, :], key_pick) > 0.5
    earlier = key_true[None, :] < query_true[:, None]
    full = earlier & pattern
    bias = jnp.where(earlier & ~pattern & flag, 0.0, NEG).T.astype(jnp.bfloat16)
    slot = jnp.arange(key_true.shape[0], dtype=jnp.int32)
    upto = (slot[:, None] <= slot[None, :]).astype(jnp.bfloat16)
    rank = jnp.dot(full.astype(jnp.bfloat16), upto, preferred_element_type=jnp.float32).astype(jnp.int32) - 1
    hit = full[:, None, :] & (rank[:, None, :] == slot[None, :, None])
    lists = jnp.sum(jnp.where(hit, slot[None, None, :], 0), axis=2, dtype=jnp.int32)
    counts = jnp.sum(full.astype(jnp.int32), axis=1, dtype=jnp.int32)
    same = key_true[None, :] == query_true[:, None]
    owns = jnp.sum(jnp.where(same, slot[None, :] + 1, 0), axis=1, dtype=jnp.int32) - 1
    ids = jnp.arange(counts.shape[0], dtype=jnp.int32)
    ahead = (counts[None, :] > counts[:, None]) | ((counts[None, :] == counts[:, None]) & (ids[None, :] < ids[:, None]))
    place = jnp.sum(ahead.astype(jnp.int32), axis=1, dtype=jnp.int32)
    turns = jnp.sum(jnp.where(place[None, :] == ids[:, None], ids[None, :], 0), axis=1, dtype=jnp.int32)
    lane = jnp.arange(HEAD, dtype=jnp.int32)[None, :]
    extra = jnp.where(lane == 0, counts[:, None], jnp.where(lane == 1, owns[:, None], jnp.where(lane == 2, turns[:, None], side)))
    return jnp.concatenate([lists, extra], axis=1), bias


TIE = 1
STEPS = (0, -1, 1, -2, 2, -3, 3, 4)


def shift(x, axis, by):
    n = lax.axis_size(axis)
    return lax.ppermute(x, axis, [(i, (i + by) % n) for i in range(n)])


def ring(kv, ours):
    half = kv.shape[0] // 2
    up, down, held = kv, kv, [kv]
    for step in range(3):
        up, down = shift(up, "z", 1), shift(down, "z", -1)
        if step == 0:
            theirs = shift(ours, "yhi", 1)
        if step == TIE:
            up, down, theirs = lax.optimization_barrier((up, down, theirs))
        held += [up, down]
    held += [shift(up[:half], "z", 1), shift(down[half:], "z", -1)]
    near, far = jnp.concatenate(held[:5]), jnp.concatenate(held[5:])
    return [near, far, shift(near, "core", 1), shift(far, "core", 1)], theirs


def pack_kernel(queries_ref, keys_ref, values_ref, out_ref):
    wide = GROUP * HEAD
    for h in range(out_ref.shape[0]):
        out_ref[h, :, :wide] = queries_ref[:, h * wide : (h + 1) * wide]
        out_ref[h, :, wide : wide + HEAD] = keys_ref[:, h * HEAD : (h + 1) * HEAD]
        out_ref[h, :, wide + HEAD :] = values_ref[:, h * HEAD : (h + 1) * HEAD]


def pack(queries, keys, values):
    vmem = pl.BlockSpec(memory_space=pltpu.VMEM)
    return pl.pallas_call(
        pack_kernel,
        out_shape=jax.ShapeDtypeStruct((keys.shape[1] // HEAD, SPAN, (GROUP + 2) * HEAD), jnp.bfloat16),
        in_specs=[vmem] * 3,
        out_specs=vmem,
        compiler_params=pltpu.CompilerParams(vmem_limit_bytes=16 * 1024 * 1024),
    )(queries, keys, values)


def per_device(queries, keys, values, span_order, block_pattern, summary_flag):
    heads = keys.shape[1] // HEAD
    pieces = lax.axis_size("yhi")
    packed = pack(queries, keys, values)
    packed = lax.all_to_all(packed, HEADS, split_axis=0, concat_axis=0, tiled=True)
    ours, kv = packed[:, :, : GROUP * HEAD], packed[:, :, GROUP * HEAD :]

    order = span_order.reshape(2, 2, 2, lax.axis_size("z"), 2, 2)
    query_true = lax.dynamic_index_in_dim(order, lax.axis_index("z"), 3, keepdims=False)
    query_true = lax.dynamic_index_in_dim(query_true, lax.axis_index("core"), 1, keepdims=False)
    query_true = query_true.transpose(0, 1, 3, 2).reshape(-1)
    key_true = lax.dynamic_index_in_dim(order, lax.axis_index("yhi"), 4, keepdims=False)
    key_true = key_true.transpose(1, 3, 0, 2, 4)
    core, depth, z = lax.axis_index("core"), lax.axis_size("z"), lax.axis_index("z")
    key_true = jnp.take(key_true, (core + jnp.arange(2, dtype=jnp.int32)) % 2, axis=0)
    key_true = jnp.take(key_true, (z + jnp.array(STEPS, jnp.int32) + depth) % depth, axis=1).reshape(-1)
    table, mask = tables(query_true, key_true, lax.axis_index("yhi"), block_pattern, summary_flag)

    ours, kv, table, mask = lax.optimization_barrier((ours, kv, table, mask))
    pieces_of_keys, theirs = ring(kv, ours)
    parts = attend(table, mask, ours, theirs, pieces_of_keys)
    parts = lax.all_to_all(parts, HEADS + ("yhi",), split_axis=0, concat_axis=0, tiled=True)
    return combine(parts, pieces)


def solution(mesh):
    fine = Mesh(mesh.devices.reshape(2, 2, 2, 8, 2, 2), ALL)
    return jax.shard_map(
        per_device,
        mesh=fine,
        in_specs=(P(ALL, None), P(ALL, None), P(ALL, None), P(), P(), P()),
        out_specs=P(ALL, None),
        check_vma=False,
    )
```

```python
import math

import jax
import jax.numpy as jnp
from jax import lax
from jax.experimental import pallas as pl
from jax.experimental.pallas import tpu as pltpu
from jax.sharding import Mesh
from jax.sharding import PartitionSpec as P

HEAD = 128
GROUP = 4
SPAN = 56
PADDED = 64
ROWS = GROUP * SPAN
EXTRA = 16
BATCH = 8
TOGETHER = 4
NEG = -1e30
LOG2E = math.log2(math.e)
SCORE_SCALE = LOG2E / math.sqrt(HEAD)
SUMMARY_BIAS = math.log2(SPAN)

HEADS = ("xhi", "xlo", "ylo")
ALL = ("xhi", "core", "xlo", "z", "yhi", "ylo")


def nt_dot(a, b):
    return lax.dot_general(a, b, (((1,), (1,)), ((), ())), preferred_element_type=jnp.float32)


def attend_kernel(
    table_ref, mask_ref, ours_ref, theirs_ref, *refs, pieces, together
):
    piece_refs, (out_ref, kv_ref, sums, base, held, turned) = refs[:pieces], refs[pieces:]
    key_spans = kv_ref.shape[0]
    query_spans = out_ref.shape[0]
    count_at, own_at, turn_at, side_at = range(key_spans, key_spans + 4)
    side = table_ref[0, side_at]

    first = 0
    for piece_ref in piece_refs:

        def prepare(j, carry, piece_ref=piece_ref, first=first):
            block = piece_ref[j]
            kv_ref[first + j] = block
            sums[pl.ds(first + j, 1), :] = jnp.sum(block.astype(jnp.float32), axis=0, keepdims=True)
            return carry

        lax.fori_loop(0, piece_ref.shape[0], prepare, 0, unroll=8)
        first += piece_ref.shape[0]
    summary = (sums[...] / math.sqrt(SPAN)).astype(jnp.bfloat16)

    summary_keys = jnp.concatenate([summary[:, :HEAD], mask_ref[...]], axis=1)
    none = jnp.zeros((PADDED, HEAD), jnp.bfloat16)
    span_row = lax.broadcasted_iota(jnp.int32, (HEAD, ROWS), 0)
    gap = jnp.zeros((PADDED - SPAN, HEAD), jnp.bfloat16)
    blank = jnp.zeros((PADDED - SPAN, ROWS), jnp.float32)
    key = lax.broadcasted_iota(jnp.int32, (SPAN, ROWS), 0)
    query = lax.broadcasted_iota(jnp.int32, (SPAN, ROWS), 1) % SPAN
    causal = jnp.where(key <= query, 0.0, NEG)
    eye = (
        lax.broadcasted_iota(jnp.int32, (ROWS, ROWS), 0) == lax.broadcasted_iota(jnp.int32, (ROWS, ROWS), 1)
    ).astype(jnp.bfloat16)

    def pile(slots, lanes):
        blocks = []
        for slot in slots:
            blocks += [kv_ref[slot, :, lanes], gap]
        return jnp.concatenate(blocks, axis=0)

    def high(x):
        return jnp.max(x.reshape(x.shape[0] // 8, 8, x.shape[1]), axis=0)

    def add(x):
        return jnp.sum(x.reshape(x.shape[0] // 8, 8, x.shape[1]), axis=0)

    def mixed_by(values, weight):
        return lax.dot_general(
            values, weight.astype(jnp.bfloat16), (((0,), (0,)), ((), ())), preferred_element_type=jnp.float32
        )

    key_lanes, value_lanes = pl.ds(0, HEAD), pl.ds(HEAD, HEAD)

    def some_spans(i, carry):
        spans = [table_ref[i * together + u, turn_at] for u in range(together)]
        counts = [table_ref[s, count_at] for s in spans]
        owns = [table_ref[s, own_at] for s in spans]
        most = counts[0]
        for c in counts[1:]:
            most = jnp.maximum(most, c)
        batches = (most + BATCH - 1) // BATCH

        for u, s in enumerate(spans):
            rows = jnp.where(s % 2 == side, ours_ref[s // 2], theirs_ref[s // 2]).astype(jnp.float32)
            rows = jnp.concatenate([rows[:, g * HEAD : (g + 1) * HEAD] for g in range(GROUP)], axis=0)
            turned[u, :HEAD] = rows.astype(jnp.bfloat16).T
            turned[u, HEAD:] = (span_row == s).astype(jnp.bfloat16)

        peaks = []
        for u, s in enumerate(spans):
            keys = jnp.concatenate([summary_keys, jnp.concatenate([pile([jnp.maximum(owns[u], 0)], key_lanes), none], axis=1)], axis=0)
            scores = jnp.dot(keys, turned[u], preferred_element_type=jnp.float32) * SCORE_SCALE
            far = scores[:key_spans] + SUMMARY_BIAS
            near = scores[key_spans : key_spans + SPAN] + (causal + jnp.where(owns[u] >= 0, 0.0, NEG))
            base[u, :key_spans] = far
            base[u, key_spans:] = near
            peaks.append(jnp.maximum(high(far), high(near)))

        def score(t, peaks):
            new = []
            for u, s in enumerate(spans):
                keys = pile([table_ref[s, t * BATCH + k] for k in range(BATCH)], key_lanes)
                scores = jnp.dot(keys, turned[u, :HEAD], preferred_element_type=jnp.float32) * SCORE_SCALE
                peak = peaks[u]
                for k in range(BATCH):
                    part = scores[k * PADDED : k * PADDED + SPAN]
                    part = part + jnp.where(t * BATCH + k < counts[u], 0.0, NEG)
                    held[u, t, k * SPAN : (k + 1) * SPAN] = part
                    peak = jnp.maximum(peak, high(part))
                new.append(peak)
            return tuple(new)

        peaks = lax.fori_loop(0, batches, score, tuple(peaks))
        peaks = [jnp.max(peak, axis=0, keepdims=True) for peak in peaks]

        state = []
        for u, s in enumerate(spans):
            weight = jnp.exp2(base[u] - peaks[u])
            values = jnp.concatenate([summary[:, HEAD:], pile([jnp.maximum(owns[u], 0)], value_lanes)], axis=0)
            total = add(weight)
            state.append((total, mixed_by(values, jnp.concatenate([weight, blank], axis=0))))

        def mix(t, state):
            new = []
            for u, s in enumerate(spans):
                total, mixed = state[u]
                values = pile([table_ref[s, t * BATCH + k] for k in range(BATCH)], value_lanes)
                weight = jnp.exp2(held[u, t] - peaks[u])
                total = total + add(weight)
                parts = []
                for k in range(BATCH):
                    parts += [weight[k * SPAN : (k + 1) * SPAN], blank]
                new.append((total, mixed + mixed_by(values, jnp.concatenate(parts, axis=0))))
            return tuple(new)

        state = lax.fori_loop(0, batches, mix, tuple(state))
        for u, s in enumerate(spans):
            total, mixed = state[u]
            total = jnp.sum(total, axis=0, keepdims=True)
            out_ref[s, :ROWS, :] = (mixed / total).astype(jnp.bfloat16).T
            level = peaks[u] + jnp.log2(total)
            first = level.astype(jnp.bfloat16).astype(jnp.float32)
            second = (level - first).astype(jnp.bfloat16).astype(jnp.float32)
            rows = jnp.concatenate([first, second, level - first - second, blank[:5]], axis=0)
            rows = jnp.concatenate([rows, jnp.zeros((8, 2 * HEAD - ROWS), jnp.float32)], axis=1)
            rows = jnp.concatenate([rows[:, :HEAD], rows[:, HEAD:]], axis=0)
            out_ref[s, ROWS:, :] = rows.astype(jnp.bfloat16)
        return carry

    lax.fori_loop(0, query_spans // together, some_spans, 0)


def attend(table, mask, ours, theirs, pieces):
    query_spans, key_spans = table.shape[0], sum(piece.shape[0] for piece in pieces)
    vmem = pl.BlockSpec(memory_space=pltpu.VMEM)
    smem = pl.BlockSpec(memory_space=pltpu.SMEM)

    def kernel(*refs):
        attend_kernel(*refs, pieces=len(pieces), together=TOGETHER)

    return pl.pallas_call(
        kernel,
        out_shape=jax.ShapeDtypeStruct((query_spans, ROWS + EXTRA, HEAD), jnp.bfloat16),
        in_specs=[smem] + [vmem] * (3 + len(pieces)),
        out_specs=vmem,
        scratch_shapes=[
            pltpu.VMEM((key_spans, SPAN, 2 * HEAD), jnp.bfloat16),
            pltpu.VMEM((key_spans, 2 * HEAD), jnp.float32),
            pltpu.VMEM((TOGETHER, key_spans + SPAN, ROWS), jnp.float32),
            pltpu.VMEM((TOGETHER, key_spans // BATCH, BATCH * SPAN, ROWS), jnp.float32),
            pltpu.VMEM((TOGETHER, 2 * HEAD, ROWS), jnp.bfloat16),
        ],
        compiler_params=pltpu.CompilerParams(vmem_limit_bytes=48 * 1024 * 1024),
    )(table, mask, ours, theirs, *pieces)


def combine_kernel(parts_ref, out_ref, *, pieces):
    heads = parts_ref.shape[0] // pieces
    three = (lax.broadcasted_iota(jnp.int32, (8, HEAD), 0) < 3).astype(jnp.bfloat16)

    def spread(rows):
        return lax.dot_general(rows, three, (((0,), (0,)), ((), ())), preferred_element_type=jnp.float32)

    for h in range(heads):
        levels = []
        for y in range(pieces):
            tail = parts_ref[h * pieces + y, ROWS:, :].astype(jnp.float32)
            both = [spread(tail[k * 8 : k * 8 + 8].astype(jnp.bfloat16)) for k in range(2)]
            levels.append(jnp.concatenate(both, axis=0)[:ROWS])
        peak = levels[0]
        for level in levels[1:]:
            peak = jnp.maximum(peak, level)
        total = jnp.zeros_like(peak)
        mixed = jnp.zeros_like(peak)
        for y in range(pieces):
            weight = jnp.exp2(levels[y] - peak)
            total = total + weight
            mixed = mixed + weight * parts_ref[h * pieces + y, :ROWS, :].astype(jnp.float32)
        mixed = (mixed / total)
        for g in range(GROUP):
            at = (h * GROUP + g) * HEAD
            out_ref[:, at : at + HEAD] = mixed[g * SPAN : (g + 1) * SPAN].astype(jnp.bfloat16)


def combine(parts, pieces):
    heads = parts.shape[0] // pieces
    vmem = pl.BlockSpec(memory_space=pltpu.VMEM)

    def kernel(parts_ref, out_ref):
        combine_kernel(parts_ref, out_ref, pieces=pieces)

    return pl.pallas_call(
        kernel,
        out_shape=jax.ShapeDtypeStruct((SPAN, heads * GROUP * HEAD), jnp.bfloat16),
        in_specs=[vmem],
        out_specs=vmem,
        compiler_params=pltpu.CompilerParams(vmem_limit_bytes=32 * 1024 * 1024),
    )(parts)


def tables(query_true, key_true, side, block_pattern, summary_flag):
    spans = block_pattern.shape[0]
    ids = jnp.arange(spans, dtype=jnp.int32)
    query_pick = (query_true[:, None] == ids[None, :]).astype(jnp.bfloat16)
    key_pick = (key_true[:, None] == ids[None, :]).astype(jnp.bfloat16)
    rows = jnp.dot(query_pick, block_pattern.astype(jnp.bfloat16), preferred_element_type=jnp.float32)
    pattern = nt_dot(rows.astype(jnp.bfloat16), key_pick) > 0.5
    flag = nt_dot((summary_flag == 1).astype(jnp.bfloat16)[None, :], key_pick) > 0.5
    earlier = key_true[None, :] < query_true[:, None]
    full = earlier & pattern
    bias = jnp.where(earlier & ~pattern & flag, 0.0, NEG).T.astype(jnp.bfloat16)
    slot = jnp.arange(key_true.shape[0], dtype=jnp.int32)
    upto = (slot[:, None] <= slot[None, :]).astype(jnp.bfloat16)
    rank = jnp.dot(full.astype(jnp.bfloat16), upto, preferred_element_type=jnp.float32).astype(jnp.int32) - 1
    hit = full[:, None, :] & (rank[:, None, :] == slot[None, :, None])
    lists = jnp.sum(jnp.where(hit, slot[None, None, :], 0), axis=2, dtype=jnp.int32)
    counts = jnp.sum(full.astype(jnp.int32), axis=1, dtype=jnp.int32)
    same = key_true[None, :] == query_true[:, None]
    owns = jnp.sum(jnp.where(same, slot[None, :] + 1, 0), axis=1, dtype=jnp.int32) - 1
    ids = jnp.arange(counts.shape[0], dtype=jnp.int32)
    ahead = (counts[None, :] > counts[:, None]) | ((counts[None, :] == counts[:, None]) & (ids[None, :] < ids[:, None]))
    place = jnp.sum(ahead.astype(jnp.int32), axis=1, dtype=jnp.int32)
    turns = jnp.sum(jnp.where(place[None, :] == ids[:, None], ids[None, :], 0), axis=1, dtype=jnp.int32)
    lane = jnp.arange(HEAD, dtype=jnp.int32)[None, :]
    extra = jnp.where(lane == 0, counts[:, None], jnp.where(lane == 1, owns[:, None], jnp.where(lane == 2, turns[:, None], side)))
    bias = jnp.concatenate([bias, jnp.zeros((bias.shape[0], HEAD - bias.shape[1]), jnp.bfloat16)], axis=1)
    return jnp.concatenate([lists, extra], axis=1), bias


TIE = 1
STEPS = (0, -1, 1, -2, 2, -3, 3, 4)


def shift(x, axis, by):
    n = lax.axis_size(axis)
    return lax.ppermute(x, axis, [(i, (i + by) % n) for i in range(n)])


def ring(kv, ours):
    half = kv.shape[0] // 2
    up, down, held = kv, kv, [kv]
    for step in range(3):
        up, down = shift(up, "z", 1), shift(down, "z", -1)
        if step == 0:
            theirs = shift(ours, "yhi", 1)
        if step == TIE:
            up, down, theirs = lax.optimization_barrier((up, down, theirs))
        held += [up, down]
        if step == 1:
            far_up, far_down = up[:half], down[half:]
    held += [shift(far_up, "z", 2), shift(far_down, "z", -2)]
    near, far = jnp.concatenate(held[:5]), jnp.concatenate(held[5:])
    return [near, far, shift(near, "core", 1), shift(far, "core", 1)], theirs


def pack_kernel(queries_ref, keys_ref, values_ref, out_ref, queries, keys, values, done):
    wide = GROUP * HEAD
    copies = [
        pltpu.make_async_copy(keys_ref, keys, done.at[0]),
        pltpu.make_async_copy(values_ref, values, done.at[1]),
        pltpu.make_async_copy(queries_ref, queries, done.at[2]),
    ]
    for copy in copies:
        copy.start()
    for copy in copies:
        copy.wait()
    for h in range(out_ref.shape[0]):
        out_ref[h, :, :wide] = queries[:, h * wide : (h + 1) * wide]
        out_ref[h, :, wide : wide + HEAD] = keys[:, h * HEAD : (h + 1) * HEAD]
        out_ref[h, :, wide + HEAD :] = values[:, h * HEAD : (h + 1) * HEAD]


def pack(queries, keys, values):
    heads = keys.shape[1] // HEAD
    return pl.pallas_call(
        pack_kernel,
        out_shape=jax.ShapeDtypeStruct((heads, SPAN, (GROUP + 2) * HEAD), jnp.bfloat16),
        in_specs=[pl.BlockSpec(memory_space=pl.ANY)] * 3,
        out_specs=pl.BlockSpec(memory_space=pltpu.VMEM),
        scratch_shapes=[pltpu.VMEM(x.shape, x.dtype) for x in (queries, keys, values)]
        + [pltpu.SemaphoreType.DMA((3,))],
        compiler_params=pltpu.CompilerParams(vmem_limit_bytes=60 * 1024 * 1024),
    )(queries, keys, values)


def per_device(queries, keys, values, span_order, block_pattern, summary_flag):
    heads = keys.shape[1] // HEAD
    pieces = lax.axis_size("yhi")
    packed = pack(queries, keys, values)
    packed = lax.all_to_all(packed, HEADS, split_axis=0, concat_axis=0, tiled=True)
    ours, kv = packed[:, :, : GROUP * HEAD], packed[:, :, GROUP * HEAD :]

    order = span_order.reshape(2, 2, 2, lax.axis_size("z"), 2, 2)
    query_true = lax.dynamic_index_in_dim(order, lax.axis_index("z"), 3, keepdims=False)
    query_true = lax.dynamic_index_in_dim(query_true, lax.axis_index("core"), 1, keepdims=False)
    query_true = query_true.transpose(0, 1, 3, 2).reshape(-1)
    key_true = lax.dynamic_index_in_dim(order, lax.axis_index("yhi"), 4, keepdims=False)
    key_true = key_true.transpose(1, 3, 0, 2, 4)
    core, depth, z = lax.axis_index("core"), lax.axis_size("z"), lax.axis_index("z")
    key_true = jnp.take(key_true, (core + jnp.arange(2, dtype=jnp.int32)) % 2, axis=0)
    key_true = jnp.take(key_true, (z + jnp.array(STEPS, jnp.int32) + depth) % depth, axis=1).reshape(-1)
    table, mask = tables(query_true, key_true, lax.axis_index("yhi"), block_pattern, summary_flag)

    ours, kv, table, mask = lax.optimization_barrier((ours, kv, table, mask))
    pieces_of_keys, theirs = ring(kv, ours)
    parts = attend(table, mask, ours, theirs, pieces_of_keys)
    parts = lax.all_to_all(parts, HEADS + ("yhi",), split_axis=0, concat_axis=0, tiled=True)
    return combine(parts, pieces)


def solution(mesh):
    fine = Mesh(mesh.devices.reshape(2, 2, 2, 8, 2, 2), ALL)
    return jax.shard_map(
        per_device,
        mesh=fine,
        in_specs=(P(ALL, None), P(ALL, None), P(ALL, None), P(), P(), P()),
        out_specs=P(ALL, None),
        check_vma=False,
    )
```

```python
import math

import jax
import jax.numpy as jnp
from jax import lax
from jax.experimental import pallas as pl
from jax.experimental.pallas import tpu as pltpu
from jax.sharding import Mesh
from jax.sharding import PartitionSpec as P

HEAD = 128
GROUP = 4
SPAN = 56
PADDED = 64
ROWS = GROUP * SPAN
EXTRA = 16
BATCH = 8
TOGETHER = 4
NEG = -1e30
LOG2E = math.log2(math.e)
SCORE_SCALE = LOG2E / math.sqrt(HEAD)
SUMMARY_BIAS = math.log2(SPAN)

HEADS = ("xhi", "xlo", "ylo")
ALL = ("xhi", "core", "xlo", "z", "yhi", "ylo")


def nt_dot(a, b):
    return lax.dot_general(a, b, (((1,), (1,)), ((), ())), preferred_element_type=jnp.float32)


def attend_kernel(
    table_ref, mask_ref, ours_ref, theirs_ref, *refs, pieces, together
):
    piece_refs, (out_ref, kv_ref, sums, base, held, turned) = refs[:pieces], refs[pieces:]
    key_spans = kv_ref.shape[0]
    query_spans = out_ref.shape[0]
    count_at, own_at, turn_at, side_at = range(key_spans, key_spans + 4)
    side = table_ref[0, side_at]

    first = 0
    for piece_ref in piece_refs:

        def prepare(j, carry, piece_ref=piece_ref, first=first):
            block = piece_ref[j]
            kv_ref[first + j] = block
            sums[pl.ds(first + j, 1), :] = jnp.sum(block.astype(jnp.float32), axis=0, keepdims=True)
            return carry

        lax.fori_loop(0, piece_ref.shape[0], prepare, 0, unroll=8)
        first += piece_ref.shape[0]
    summary = (sums[...] / math.sqrt(SPAN)).astype(jnp.bfloat16)

    summary_keys = jnp.concatenate([summary[:, :HEAD], mask_ref[...]], axis=1)
    none = jnp.zeros((PADDED, HEAD), jnp.bfloat16)
    span_row = lax.broadcasted_iota(jnp.int32, (HEAD, ROWS), 0)
    gap = jnp.zeros((PADDED - SPAN, HEAD), jnp.bfloat16)
    blank = jnp.zeros((PADDED - SPAN, ROWS), jnp.float32)
    key = lax.broadcasted_iota(jnp.int32, (SPAN, ROWS), 0)
    query = lax.broadcasted_iota(jnp.int32, (SPAN, ROWS), 1) % SPAN
    causal = jnp.where(key <= query, 0.0, NEG)
    eye = (
        lax.broadcasted_iota(jnp.int32, (ROWS, ROWS), 0) == lax.broadcasted_iota(jnp.int32, (ROWS, ROWS), 1)
    ).astype(jnp.bfloat16)

    def pile(slots, lanes):
        blocks = []
        for slot in slots:
            blocks += [kv_ref[slot, :, lanes], gap]
        return jnp.concatenate(blocks, axis=0)

    def high(x):
        return jnp.max(x.reshape(x.shape[0] // 8, 8, x.shape[1]), axis=0)

    def add(x):
        return jnp.sum(x.reshape(x.shape[0] // 8, 8, x.shape[1]), axis=0)

    def mixed_by(values, weight):
        return lax.dot_general(
            values, weight.astype(jnp.bfloat16), (((0,), (0,)), ((), ())), preferred_element_type=jnp.float32
        )

    key_lanes, value_lanes = pl.ds(0, HEAD), pl.ds(HEAD, HEAD)

    def some_spans(i, carry):
        spans = [table_ref[i * together + u, turn_at] for u in range(together)]
        counts = [table_ref[s, count_at] for s in spans]
        owns = [table_ref[s, own_at] for s in spans]
        most = counts[0]
        for c in counts[1:]:
            most = jnp.maximum(most, c)
        batches = (most + BATCH - 1) // BATCH

        for u, s in enumerate(spans):
            rows = jnp.where(s % 2 == side, ours_ref[s // 2], theirs_ref[s // 2]).astype(jnp.float32)
            rows = jnp.concatenate([rows[:, g * HEAD : (g + 1) * HEAD] for g in range(GROUP)], axis=0)
            turned[u, :HEAD] = rows.astype(jnp.bfloat16).T
            turned[u, HEAD:] = (span_row == s).astype(jnp.bfloat16)

        peaks = []
        for u, s in enumerate(spans):
            keys = jnp.concatenate([summary_keys, jnp.concatenate([pile([jnp.maximum(owns[u], 0)], key_lanes), none], axis=1)], axis=0)
            scores = jnp.dot(keys, turned[u], preferred_element_type=jnp.float32) * SCORE_SCALE
            far = scores[:key_spans] + SUMMARY_BIAS
            near = scores[key_spans : key_spans + SPAN] + (causal + jnp.where(owns[u] >= 0, 0.0, NEG))
            base[u, :key_spans] = far
            base[u, key_spans:] = near
            peaks.append(jnp.maximum(high(far), high(near)))

        def score(t, peaks):
            new = []
            for u, s in enumerate(spans):
                keys = pile([table_ref[s, t * BATCH + k] for k in range(BATCH)], key_lanes)
                scores = jnp.dot(keys, turned[u, :HEAD], preferred_element_type=jnp.float32) * SCORE_SCALE
                peak = peaks[u]
                for k in range(BATCH):
                    part = scores[k * PADDED : k * PADDED + SPAN]
                    part = part + jnp.where(t * BATCH + k < counts[u], 0.0, NEG)
                    held[u, t, k * SPAN : (k + 1) * SPAN] = part
                    peak = jnp.maximum(peak, high(part))
                new.append(peak)
            return tuple(new)

        peaks = lax.fori_loop(1, batches, score, score(0, tuple(peaks)))
        peaks = [jnp.max(peak, axis=0, keepdims=True) for peak in peaks]

        state = []
        for u, s in enumerate(spans):
            weight = jnp.exp2(base[u] - peaks[u])
            values = jnp.concatenate([summary[:, HEAD:], pile([jnp.maximum(owns[u], 0)], value_lanes)], axis=0)
            total = add(weight)
            state.append((total, mixed_by(values, jnp.concatenate([weight, blank], axis=0))))

        def mix(t, state):
            new = []
            for u, s in enumerate(spans):
                total, mixed = state[u]
                values = pile([table_ref[s, t * BATCH + k] for k in range(BATCH)], value_lanes)
                weight = jnp.exp2(held[u, t] - peaks[u])
                total = total + add(weight)
                parts = []
                for k in range(BATCH):
                    parts += [weight[k * SPAN : (k + 1) * SPAN], blank]
                new.append((total, mixed + mixed_by(values, jnp.concatenate(parts, axis=0))))
            return tuple(new)

        state = lax.fori_loop(1, batches, mix, mix(0, tuple(state)))
        for u, s in enumerate(spans):
            total, mixed = state[u]
            total = jnp.sum(total, axis=0, keepdims=True)
            out_ref[s, :ROWS, :] = (mixed * (1.0 / total)).astype(jnp.bfloat16).T
            level = peaks[u] + jnp.log2(total)
            first = level.astype(jnp.bfloat16).astype(jnp.float32)
            second = (level - first).astype(jnp.bfloat16).astype(jnp.float32)
            rows = jnp.concatenate([first, second, level - first - second, blank[:5]], axis=0)
            rows = jnp.concatenate([rows, jnp.zeros((8, 2 * HEAD - ROWS), jnp.float32)], axis=1)
            rows = jnp.concatenate([rows[:, :HEAD], rows[:, HEAD:]], axis=0)
            out_ref[s, ROWS:, :] = rows.astype(jnp.bfloat16)
        return carry

    lax.fori_loop(0, query_spans // together, some_spans, 0)


def attend(table, mask, ours, theirs, pieces):
    query_spans, key_spans = table.shape[0], sum(piece.shape[0] for piece in pieces)
    vmem = pl.BlockSpec(memory_space=pltpu.VMEM)
    smem = pl.BlockSpec(memory_space=pltpu.SMEM)

    def kernel(*refs):
        attend_kernel(*refs, pieces=len(pieces), together=TOGETHER)

    return pl.pallas_call(
        kernel,
        out_shape=jax.ShapeDtypeStruct((query_spans, ROWS + EXTRA, HEAD), jnp.bfloat16),
        in_specs=[smem] + [vmem] * (3 + len(pieces)),
        out_specs=vmem,
        scratch_shapes=[
            pltpu.VMEM((key_spans, SPAN, 2 * HEAD), jnp.bfloat16),
            pltpu.VMEM((key_spans, 2 * HEAD), jnp.float32),
            pltpu.VMEM((TOGETHER, key_spans + SPAN, ROWS), jnp.float32),
            pltpu.VMEM((TOGETHER, key_spans // BATCH, BATCH * SPAN, ROWS), jnp.float32),
            pltpu.VMEM((TOGETHER, 2 * HEAD, ROWS), jnp.bfloat16),
        ],
        compiler_params=pltpu.CompilerParams(vmem_limit_bytes=48 * 1024 * 1024),
    )(table, mask, ours, theirs, *pieces)


def combine_kernel(parts_ref, out_ref, *, pieces):
    heads = parts_ref.shape[0] // pieces
    three = (lax.broadcasted_iota(jnp.int32, (8, HEAD), 0) < 3).astype(jnp.bfloat16)
    rest = jnp.zeros((5, HEAD), jnp.float32)

    def spread(row):
        first = row.astype(jnp.bfloat16).astype(jnp.float32)
        second = (row - first).astype(jnp.bfloat16).astype(jnp.float32)
        rows = jnp.concatenate([first, second, row - first - second, rest], axis=0).astype(jnp.bfloat16)
        return lax.dot_general(rows, three, (((0,), (0,)), ((), ())), preferred_element_type=jnp.float32)

    for h in range(heads):
        shares = [[] for _ in range(pieces)]
        tails = [parts_ref[h * pieces + y, ROWS:, :].astype(jnp.float32) for y in range(pieces)]
        for k in range(0, 16, 8):
            levels = [tail[k : k + 1] + tail[k + 1 : k + 2] + tail[k + 2 : k + 3] for tail in tails]
            peak = levels[0]
            for level in levels[1:]:
                peak = jnp.maximum(peak, level)
            weights = [jnp.exp2(level - peak) for level in levels]
            scale = 1.0 / sum(weights)
            for y in range(pieces):
                shares[y].append(spread(weights[y] * scale))
        mixed = jnp.zeros((ROWS, HEAD), jnp.float32)
        for y in range(pieces):
            share = jnp.concatenate(shares[y], axis=0)[:ROWS]
            mixed = mixed + share * parts_ref[h * pieces + y, :ROWS, :].astype(jnp.float32)
        for g in range(GROUP):
            at = (h * GROUP + g) * HEAD
            out_ref[:, at : at + HEAD] = mixed[g * SPAN : (g + 1) * SPAN].astype(jnp.bfloat16)


def combine(parts, pieces):
    heads = parts.shape[0] // pieces
    vmem = pl.BlockSpec(memory_space=pltpu.VMEM)

    def kernel(parts_ref, out_ref):
        combine_kernel(parts_ref, out_ref, pieces=pieces)

    return pl.pallas_call(
        kernel,
        out_shape=jax.ShapeDtypeStruct((SPAN, heads * GROUP * HEAD), jnp.bfloat16),
        in_specs=[vmem],
        out_specs=vmem,
        compiler_params=pltpu.CompilerParams(vmem_limit_bytes=32 * 1024 * 1024),
    )(parts)


def tables(query_true, key_true, side, block_pattern, summary_flag):
    spans = block_pattern.shape[0]
    ids = jnp.arange(spans, dtype=jnp.int32)
    query_pick = (query_true[:, None] == ids[None, :]).astype(jnp.bfloat16)
    key_pick = (key_true[:, None] == ids[None, :]).astype(jnp.bfloat16)
    rows = jnp.dot(query_pick, block_pattern.astype(jnp.bfloat16), preferred_element_type=jnp.float32)
    pattern = nt_dot(rows.astype(jnp.bfloat16), key_pick) > 0.5
    flag = nt_dot((summary_flag == 1).astype(jnp.bfloat16)[None, :], key_pick) > 0.5
    earlier = key_true[None, :] < query_true[:, None]
    full = earlier & pattern
    bias = jnp.where(earlier & ~pattern & flag, 0.0, NEG).T.astype(jnp.bfloat16)
    slot = jnp.arange(key_true.shape[0], dtype=jnp.int32)
    upto = (slot[:, None] <= slot[None, :]).astype(jnp.bfloat16)
    rank = jnp.dot(full.astype(jnp.bfloat16), upto, preferred_element_type=jnp.float32).astype(jnp.int32) - 1
    hit = full[:, None, :] & (rank[:, None, :] == slot[None, :, None])
    lists = jnp.sum(jnp.where(hit, slot[None, None, :], 0), axis=2, dtype=jnp.int32)
    counts = jnp.sum(full.astype(jnp.int32), axis=1, dtype=jnp.int32)
    same = key_true[None, :] == query_true[:, None]
    owns = jnp.sum(jnp.where(same, slot[None, :] + 1, 0), axis=1, dtype=jnp.int32) - 1
    ids = jnp.arange(counts.shape[0], dtype=jnp.int32)
    ahead = (counts[None, :] > counts[:, None]) | ((counts[None, :] == counts[:, None]) & (ids[None, :] < ids[:, None]))
    place = jnp.sum(ahead.astype(jnp.int32), axis=1, dtype=jnp.int32)
    turns = jnp.sum(jnp.where(place[None, :] == ids[:, None], ids[None, :], 0), axis=1, dtype=jnp.int32)
    lane = jnp.arange(HEAD, dtype=jnp.int32)[None, :]
    extra = jnp.where(lane == 0, counts[:, None], jnp.where(lane == 1, owns[:, None], jnp.where(lane == 2, turns[:, None], side)))
    bias = jnp.concatenate([bias, jnp.zeros((bias.shape[0], HEAD - bias.shape[1]), jnp.bfloat16)], axis=1)
    return jnp.concatenate([lists, extra], axis=1), bias


TIE = 1
STEPS = (0, -1, 1, -2, 2, -3, 3, 4)


def shift(x, axis, by):
    n = lax.axis_size(axis)
    return lax.ppermute(x, axis, [(i, (i + by) % n) for i in range(n)])


def ring(kv, ours):
    half = kv.shape[0] // 2
    up, down, held = kv, kv, [kv]
    for step in range(3):
        up, down = shift(up, "z", 1), shift(down, "z", -1)
        if step == 0:
            theirs = shift(ours, "yhi", 1)
        if step == TIE:
            up, down, theirs = lax.optimization_barrier((up, down, theirs))
        held += [up, down]
        if step == 1:
            far_up, far_down = up[:half], down[half:]
    held += [shift(far_up, "z", 2), shift(far_down, "z", -2)]
    near, far = jnp.concatenate(held[:5]), jnp.concatenate(held[5:])
    return [near, far, shift(near, "core", 1), shift(far, "core", 1)], theirs


def pack_kernel(queries_ref, keys_ref, values_ref, out_ref, queries, keys, values, done):
    wide = GROUP * HEAD
    copies = [
        pltpu.make_async_copy(keys_ref, keys, done.at[0]),
        pltpu.make_async_copy(values_ref, values, done.at[1]),
        pltpu.make_async_copy(queries_ref, queries, done.at[2]),
    ]
    for copy in copies:
        copy.start()
    for copy in copies:
        copy.wait()
    for h in range(out_ref.shape[0]):
        out_ref[h, :, :wide] = queries[:, h * wide : (h + 1) * wide]
        out_ref[h, :, wide : wide + HEAD] = keys[:, h * HEAD : (h + 1) * HEAD]
        out_ref[h, :, wide + HEAD :] = values[:, h * HEAD : (h + 1) * HEAD]


def pack(queries, keys, values):
    heads = keys.shape[1] // HEAD
    return pl.pallas_call(
        pack_kernel,
        out_shape=jax.ShapeDtypeStruct((heads, SPAN, (GROUP + 2) * HEAD), jnp.bfloat16),
        in_specs=[pl.BlockSpec(memory_space=pl.ANY)] * 3,
        out_specs=pl.BlockSpec(memory_space=pltpu.VMEM),
        scratch_shapes=[pltpu.VMEM(x.shape, x.dtype) for x in (queries, keys, values)]
        + [pltpu.SemaphoreType.DMA((3,))],
        compiler_params=pltpu.CompilerParams(vmem_limit_bytes=60 * 1024 * 1024),
    )(queries, keys, values)


def per_device(queries, keys, values, span_order, block_pattern, summary_flag):
    heads = keys.shape[1] // HEAD
    pieces = lax.axis_size("yhi")
    packed = pack(queries, keys, values)
    packed = lax.all_to_all(packed, HEADS, split_axis=0, concat_axis=0, tiled=True)
    ours, kv = packed[:, :, : GROUP * HEAD], packed[:, :, GROUP * HEAD :]

    order = span_order.reshape(2, 2, 2, lax.axis_size("z"), 2, 2)
    query_true = lax.dynamic_index_in_dim(order, lax.axis_index("z"), 3, keepdims=False)
    query_true = lax.dynamic_index_in_dim(query_true, lax.axis_index("core"), 1, keepdims=False)
    query_true = query_true.transpose(0, 1, 3, 2).reshape(-1)
    key_true = lax.dynamic_index_in_dim(order, lax.axis_index("yhi"), 4, keepdims=False)
    key_true = key_true.transpose(1, 3, 0, 2, 4)
    core, depth, z = lax.axis_index("core"), lax.axis_size("z"), lax.axis_index("z")
    key_true = jnp.take(key_true, (core + jnp.arange(2, dtype=jnp.int32)) % 2, axis=0)
    key_true = jnp.take(key_true, (z + jnp.array(STEPS, jnp.int32) + depth) % depth, axis=1).reshape(-1)
    table, mask = tables(query_true, key_true, lax.axis_index("yhi"), block_pattern, summary_flag)

    ours, kv, table, mask = lax.optimization_barrier((ours, kv, table, mask))
    pieces_of_keys, theirs = ring(kv, ours)
    parts = attend(table, mask, ours, theirs, pieces_of_keys)
    parts = lax.all_to_all(parts, HEADS + ("yhi",), split_axis=0, concat_axis=0, tiled=True)
    return combine(parts, pieces)


def solution(mesh):
    fine = Mesh(mesh.devices.reshape(2, 2, 2, 8, 2, 2), ALL)
    return jax.shard_map(
        per_device,
        mesh=fine,
        in_specs=(P(ALL, None), P(ALL, None), P(ALL, None), P(), P(), P()),
        out_specs=P(ALL, None),
        check_vma=False,
    )
```

```python
import math

import jax
import jax.numpy as jnp
from jax import lax
from jax.experimental import pallas as pl
from jax.experimental.pallas import tpu as pltpu
from jax.sharding import Mesh
from jax.sharding import PartitionSpec as P

HEAD = 128
GROUP = 4
SPAN = 56
PADDED = 64
ROWS = GROUP * SPAN
EXTRA = 16
FIRST = 12
BATCH = 4
TOGETHER = 4
NEG = -1e30
LOG2E = math.log2(math.e)
SCORE_SCALE = LOG2E / math.sqrt(HEAD)
SUMMARY_BIAS = math.log2(SPAN)

HEADS = ("xhi", "xlo", "ylo")
ALL = ("xhi", "core", "xlo", "z", "yhi", "ylo")


def nt_dot(a, b):
    return lax.dot_general(a, b, (((1,), (1,)), ((), ())), preferred_element_type=jnp.float32)


def attend_kernel(
    table_ref, mask_ref, ours_ref, theirs_ref, *refs, pieces, together
):
    piece_refs, (out_ref, kv_ref, sums, base, held, turned) = refs[:pieces], refs[pieces:]
    key_spans = kv_ref.shape[0]
    query_spans = out_ref.shape[0]
    count_at, own_at, turn_at, side_at = range(key_spans, key_spans + 4)
    side = table_ref[0, side_at]

    first = 0
    for piece_ref in piece_refs:

        def prepare(j, carry, piece_ref=piece_ref, first=first):
            block = piece_ref[j]
            kv_ref[first + j] = block
            sums[pl.ds(first + j, 1), :] = jnp.sum(block.astype(jnp.float32), axis=0, keepdims=True)
            return carry

        lax.fori_loop(0, piece_ref.shape[0], prepare, 0, unroll=8)
        first += piece_ref.shape[0]
    summary = (sums[...] / math.sqrt(SPAN)).astype(jnp.bfloat16)

    summary_keys = jnp.concatenate([summary[:, :HEAD], mask_ref[...]], axis=1)
    none = jnp.zeros(((FIRST + 1) * PADDED, HEAD), jnp.bfloat16)
    span_row = lax.broadcasted_iota(jnp.int32, (HEAD, ROWS), 0)
    gap = jnp.zeros((PADDED - SPAN, HEAD), jnp.bfloat16)
    blank = jnp.zeros((PADDED - SPAN, ROWS), jnp.float32)
    key = lax.broadcasted_iota(jnp.int32, (SPAN, ROWS), 0)
    query = lax.broadcasted_iota(jnp.int32, (SPAN, ROWS), 1) % SPAN
    causal = jnp.where(key <= query, 0.0, NEG)
    eye = (
        lax.broadcasted_iota(jnp.int32, (ROWS, ROWS), 0) == lax.broadcasted_iota(jnp.int32, (ROWS, ROWS), 1)
    ).astype(jnp.bfloat16)

    def pile(slots, lanes):
        blocks = []
        for slot in slots:
            blocks += [kv_ref[slot, :, lanes], gap]
        return jnp.concatenate(blocks, axis=0)

    def high(x):
        return jnp.max(x.reshape(x.shape[0] // 8, 8, x.shape[1]), axis=0)

    def add(x):
        return jnp.sum(x.reshape(x.shape[0] // 8, 8, x.shape[1]), axis=0)

    def mixed_by(values, weight):
        return lax.dot_general(
            values, weight.astype(jnp.bfloat16), (((0,), (0,)), ((), ())), preferred_element_type=jnp.float32
        )

    key_lanes, value_lanes = pl.ds(0, HEAD), pl.ds(HEAD, HEAD)

    def some_spans(i, carry):
        spans = [table_ref[i * together + u, turn_at] for u in range(together)]
        counts = [table_ref[s, count_at] for s in spans]
        owns = [table_ref[s, own_at] for s in spans]
        most = counts[0]
        for c in counts[1:]:
            most = jnp.maximum(most, c)
        batches = jnp.maximum(most - FIRST + BATCH - 1, 0) // BATCH

        for u, s in enumerate(spans):
            rows = jnp.where(s % 2 == side, ours_ref[s // 2], theirs_ref[s // 2]).astype(jnp.float32)
            rows = jnp.concatenate([rows[:, g * HEAD : (g + 1) * HEAD] for g in range(GROUP)], axis=0)
            turned[u, :HEAD] = rows.astype(jnp.bfloat16).T
            turned[u, HEAD:] = (span_row == s).astype(jnp.bfloat16)

        starts = [[jnp.maximum(owns[u], 0)] + [table_ref[s, k] for k in range(FIRST)] for u, s in enumerate(spans)]
        peaks = []
        for u, s in enumerate(spans):
            blocks = pile(starts[u], key_lanes)
            keys = jnp.concatenate([summary_keys, jnp.concatenate([blocks, none], axis=1)], axis=0)
            scores = jnp.dot(keys, turned[u], preferred_element_type=jnp.float32) * SCORE_SCALE
            far = scores[:key_spans] + SUMMARY_BIAS
            base[u, :key_spans] = far
            peak = high(far)
            for k in range(FIRST + 1):
                at = key_spans + k * PADDED
                if k == 0:
                    part = scores[at : at + SPAN] + (causal + jnp.where(owns[u] >= 0, 0.0, NEG))
                else:
                    part = scores[at : at + SPAN] + jnp.where(k - 1 < counts[u], 0.0, NEG)
                base[u, key_spans + k * SPAN : key_spans + (k + 1) * SPAN] = part
                peak = jnp.maximum(peak, high(part))
            peaks.append(peak)

        def score(t, peaks):
            new = []
            for u, s in enumerate(spans):
                keys = pile([table_ref[s, FIRST + t * BATCH + k] for k in range(BATCH)], key_lanes)
                scores = jnp.dot(keys, turned[u, :HEAD], preferred_element_type=jnp.float32) * SCORE_SCALE
                peak = peaks[u]
                for k in range(BATCH):
                    part = scores[k * PADDED : k * PADDED + SPAN]
                    part = part + jnp.where(FIRST + t * BATCH + k < counts[u], 0.0, NEG)
                    held[u, t, k * SPAN : (k + 1) * SPAN] = part
                    peak = jnp.maximum(peak, high(part))
                new.append(peak)
            return tuple(new)

        peaks = lax.fori_loop(0, batches, score, tuple(peaks))
        peaks = [jnp.max(peak, axis=0, keepdims=True) for peak in peaks]

        state = []
        for u, s in enumerate(spans):
            weight = jnp.exp2(base[u] - peaks[u])
            values = jnp.concatenate([summary[:, HEAD:], pile(starts[u], value_lanes)], axis=0)
            parts = [weight[:key_spans]]
            for k in range(FIRST + 1):
                at = key_spans + k * SPAN
                parts += [weight[at : at + SPAN], blank]
            state.append((add(weight), mixed_by(values, jnp.concatenate(parts, axis=0))))

        def mix(t, state):
            new = []
            for u, s in enumerate(spans):
                total, mixed = state[u]
                values = pile([table_ref[s, FIRST + t * BATCH + k] for k in range(BATCH)], value_lanes)
                weight = jnp.exp2(held[u, t] - peaks[u])
                total = total + add(weight)
                parts = []
                for k in range(BATCH):
                    parts += [weight[k * SPAN : (k + 1) * SPAN], blank]
                new.append((total, mixed + mixed_by(values, jnp.concatenate(parts, axis=0))))
            return tuple(new)

        state = lax.fori_loop(0, batches, mix, tuple(state))
        for u, s in enumerate(spans):
            total, mixed = state[u]
            total = jnp.sum(total, axis=0, keepdims=True)
            out_ref[s, :ROWS, :] = (mixed * (1.0 / total)).astype(jnp.bfloat16).T
            level = peaks[u] + jnp.log2(total)
            first = level.astype(jnp.bfloat16).astype(jnp.float32)
            second = (level - first).astype(jnp.bfloat16).astype(jnp.float32)
            rows = jnp.concatenate([first, second, level - first - second, blank[:5]], axis=0)
            rows = jnp.concatenate([rows, jnp.zeros((8, 2 * HEAD - ROWS), jnp.float32)], axis=1)
            rows = jnp.concatenate([rows[:, :HEAD], rows[:, HEAD:]], axis=0)
            out_ref[s, ROWS:, :] = rows.astype(jnp.bfloat16)
        return carry

    lax.fori_loop(0, query_spans // together, some_spans, 0)


def attend(table, mask, ours, theirs, pieces):
    query_spans, key_spans = table.shape[0], sum(piece.shape[0] for piece in pieces)
    vmem = pl.BlockSpec(memory_space=pltpu.VMEM)
    smem = pl.BlockSpec(memory_space=pltpu.SMEM)

    def kernel(*refs):
        attend_kernel(*refs, pieces=len(pieces), together=TOGETHER)

    return pl.pallas_call(
        kernel,
        out_shape=jax.ShapeDtypeStruct((query_spans, ROWS + EXTRA, HEAD), jnp.bfloat16),
        in_specs=[smem] + [vmem] * (3 + len(pieces)),
        out_specs=vmem,
        scratch_shapes=[
            pltpu.VMEM((key_spans, SPAN, 2 * HEAD), jnp.bfloat16),
            pltpu.VMEM((key_spans, 2 * HEAD), jnp.float32),
            pltpu.VMEM((TOGETHER, key_spans + (FIRST + 1) * SPAN, ROWS), jnp.float32),
            pltpu.VMEM((TOGETHER, key_spans // BATCH, BATCH * SPAN, ROWS), jnp.float32),
            pltpu.VMEM((TOGETHER, 2 * HEAD, ROWS), jnp.bfloat16),
        ],
        compiler_params=pltpu.CompilerParams(vmem_limit_bytes=48 * 1024 * 1024),
    )(table, mask, ours, theirs, *pieces)


def combine_kernel(parts_ref, out_ref, *, pieces):
    heads = parts_ref.shape[0] // pieces
    three = (lax.broadcasted_iota(jnp.int32, (8, HEAD), 0) < 3).astype(jnp.bfloat16)
    rest = jnp.zeros((5, HEAD), jnp.float32)

    def spread(row):
        first = row.astype(jnp.bfloat16).astype(jnp.float32)
        second = (row - first).astype(jnp.bfloat16).astype(jnp.float32)
        rows = jnp.concatenate([first, second, row - first - second, rest], axis=0).astype(jnp.bfloat16)
        return lax.dot_general(rows, three, (((0,), (0,)), ((), ())), preferred_element_type=jnp.float32)

    for h in range(heads):
        shares = [[] for _ in range(pieces)]
        tails = [parts_ref[h * pieces + y, ROWS:, :].astype(jnp.float32) for y in range(pieces)]
        for k in range(0, 16, 8):
            levels = [tail[k : k + 1] + tail[k + 1 : k + 2] + tail[k + 2 : k + 3] for tail in tails]
            peak = levels[0]
            for level in levels[1:]:
                peak = jnp.maximum(peak, level)
            weights = [jnp.exp2(level - peak) for level in levels]
            scale = 1.0 / sum(weights)
            for y in range(pieces):
                shares[y].append(spread(weights[y] * scale))
        mixed = jnp.zeros((ROWS, HEAD), jnp.float32)
        for y in range(pieces):
            share = jnp.concatenate(shares[y], axis=0)[:ROWS]
            mixed = mixed + share * parts_ref[h * pieces + y, :ROWS, :].astype(jnp.float32)
        for g in range(GROUP):
            at = (h * GROUP + g) * HEAD
            out_ref[:, at : at + HEAD] = mixed[g * SPAN : (g + 1) * SPAN].astype(jnp.bfloat16)


def combine(parts, pieces):
    heads = parts.shape[0] // pieces
    vmem = pl.BlockSpec(memory_space=pltpu.VMEM)

    def kernel(parts_ref, out_ref):
        combine_kernel(parts_ref, out_ref, pieces=pieces)

    return pl.pallas_call(
        kernel,
        out_shape=jax.ShapeDtypeStruct((SPAN, heads * GROUP * HEAD), jnp.bfloat16),
        in_specs=[vmem],
        out_specs=vmem,
        compiler_params=pltpu.CompilerParams(vmem_limit_bytes=32 * 1024 * 1024),
    )(parts)


def tables(query_true, key_true, side, block_pattern, summary_flag):
    spans = block_pattern.shape[0]
    ids = jnp.arange(spans, dtype=jnp.int32)
    query_pick = (query_true[:, None] == ids[None, :]).astype(jnp.bfloat16)
    key_pick = (key_true[:, None] == ids[None, :]).astype(jnp.bfloat16)
    rows = jnp.dot(query_pick, block_pattern.astype(jnp.bfloat16), preferred_element_type=jnp.float32)
    pattern = nt_dot(rows.astype(jnp.bfloat16), key_pick) > 0.5
    flag = nt_dot((summary_flag == 1).astype(jnp.bfloat16)[None, :], key_pick) > 0.5
    earlier = key_true[None, :] < query_true[:, None]
    full = earlier & pattern
    bias = jnp.where(earlier & ~pattern & flag, 0.0, NEG).T.astype(jnp.bfloat16)
    slot = jnp.arange(key_true.shape[0], dtype=jnp.int32)
    upto = (slot[:, None] <= slot[None, :]).astype(jnp.bfloat16)
    rank = jnp.dot(full.astype(jnp.bfloat16), upto, preferred_element_type=jnp.float32).astype(jnp.int32) - 1
    hit = full[:, None, :] & (rank[:, None, :] == slot[None, :, None])
    lists = jnp.sum(jnp.where(hit, slot[None, None, :], 0), axis=2, dtype=jnp.int32)
    counts = jnp.sum(full.astype(jnp.int32), axis=1, dtype=jnp.int32)
    same = key_true[None, :] == query_true[:, None]
    owns = jnp.sum(jnp.where(same, slot[None, :] + 1, 0), axis=1, dtype=jnp.int32) - 1
    ids = jnp.arange(counts.shape[0], dtype=jnp.int32)
    ahead = (counts[None, :] > counts[:, None]) | ((counts[None, :] == counts[:, None]) & (ids[None, :] < ids[:, None]))
    place = jnp.sum(ahead.astype(jnp.int32), axis=1, dtype=jnp.int32)
    turns = jnp.sum(jnp.where(place[None, :] == ids[:, None], ids[None, :], 0), axis=1, dtype=jnp.int32)
    lane = jnp.arange(HEAD, dtype=jnp.int32)[None, :]
    extra = jnp.where(lane == 0, counts[:, None], jnp.where(lane == 1, owns[:, None], jnp.where(lane == 2, turns[:, None], side)))
    bias = jnp.concatenate([bias, jnp.zeros((bias.shape[0], HEAD - bias.shape[1]), jnp.bfloat16)], axis=1)
    return jnp.concatenate([lists, extra], axis=1), bias


TIE = 1
STEPS = (0, -1, 1, -2, 2, -3, 3, 4)


def shift(x, axis, by):
    n = lax.axis_size(axis)
    return lax.ppermute(x, axis, [(i, (i + by) % n) for i in range(n)])


def ring(kv, ours):
    half = kv.shape[0] // 2
    up, down, held = kv, kv, [kv]
    for step in range(3):
        up, down = shift(up, "z", 1), shift(down, "z", -1)
        if step == 0:
            theirs = shift(ours, "yhi", 1)
        if step == TIE:
            up, down, theirs = lax.optimization_barrier((up, down, theirs))
        held += [up, down]
        if step == 1:
            far_up, far_down = up[:half], down[half:]
    held += [shift(far_up, "z", 2), shift(far_down, "z", -2)]
    near, far = jnp.concatenate(held[:5]), jnp.concatenate(held[5:])
    return [near, far, shift(near, "core", 1), shift(far, "core", 1)], theirs


def pack_kernel(queries_ref, keys_ref, values_ref, out_ref, queries, keys, values, done):
    wide = GROUP * HEAD
    copies = [
        pltpu.make_async_copy(keys_ref, keys, done.at[0]),
        pltpu.make_async_copy(values_ref, values, done.at[1]),
        pltpu.make_async_copy(queries_ref, queries, done.at[2]),
    ]
    for copy in copies:
        copy.start()
    for copy in copies:
        copy.wait()
    for h in range(out_ref.shape[0]):
        out_ref[h, :, :wide] = queries[:, h * wide : (h + 1) * wide]
        out_ref[h, :, wide : wide + HEAD] = keys[:, h * HEAD : (h + 1) * HEAD]
        out_ref[h, :, wide + HEAD :] = values[:, h * HEAD : (h + 1) * HEAD]


def pack(queries, keys, values):
    heads = keys.shape[1] // HEAD
    return pl.pallas_call(
        pack_kernel,
        out_shape=jax.ShapeDtypeStruct((heads, SPAN, (GROUP + 2) * HEAD), jnp.bfloat16),
        in_specs=[pl.BlockSpec(memory_space=pl.ANY)] * 3,
        out_specs=pl.BlockSpec(memory_space=pltpu.VMEM),
        scratch_shapes=[pltpu.VMEM(x.shape, x.dtype) for x in (queries, keys, values)]
        + [pltpu.SemaphoreType.DMA((3,))],
        compiler_params=pltpu.CompilerParams(vmem_limit_bytes=60 * 1024 * 1024),
    )(queries, keys, values)


def per_device(queries, keys, values, span_order, block_pattern, summary_flag):
    heads = keys.shape[1] // HEAD
    pieces = lax.axis_size("yhi")
    packed = pack(queries, keys, values)
    packed = lax.all_to_all(packed, HEADS, split_axis=0, concat_axis=0, tiled=True)
    ours, kv = packed[:, :, : GROUP * HEAD], packed[:, :, GROUP * HEAD :]

    order = span_order.reshape(2, 2, 2, lax.axis_size("z"), 2, 2)
    query_true = lax.dynamic_index_in_dim(order, lax.axis_index("z"), 3, keepdims=False)
    query_true = lax.dynamic_index_in_dim(query_true, lax.axis_index("core"), 1, keepdims=False)
    query_true = query_true.transpose(0, 1, 3, 2).reshape(-1)
    key_true = lax.dynamic_index_in_dim(order, lax.axis_index("yhi"), 4, keepdims=False)
    key_true = key_true.transpose(1, 3, 0, 2, 4)
    core, depth, z = lax.axis_index("core"), lax.axis_size("z"), lax.axis_index("z")
    key_true = jnp.take(key_true, (core + jnp.arange(2, dtype=jnp.int32)) % 2, axis=0)
    key_true = jnp.take(key_true, (z + jnp.array(STEPS, jnp.int32) + depth) % depth, axis=1).reshape(-1)
    table, mask = tables(query_true, key_true, lax.axis_index("yhi"), block_pattern, summary_flag)

    ours, kv, table, mask = lax.optimization_barrier((ours, kv, table, mask))
    pieces_of_keys, theirs = ring(kv, ours)
    parts = attend(table, mask, ours, theirs, pieces_of_keys)
    parts = lax.all_to_all(parts, HEADS + ("yhi",), split_axis=0, concat_axis=0, tiled=True)
    return combine(parts, pieces)


def solution(mesh):
    fine = Mesh(mesh.devices.reshape(2, 2, 2, 8, 2, 2), ALL)
    return jax.shard_map(
        per_device,
        mesh=fine,
        in_specs=(P(ALL, None), P(ALL, None), P(ALL, None), P(), P(), P()),
        out_specs=P(ALL, None),
        check_vma=False,
    )
```
